256 devices in a mesh: uly: 4 (over x_hi, core), blk: 64 (over x_lo, y, z).
Axes of the slice: x: 4 (x_hi: 2, x_lo: 2; x = x_hi * 2 + x_lo), y: 4, z: 8, core: 2. Of those that a mesh axis runs over, the one named last changes fastest.
Arguments:
- queries: bfloat16 [8192, 3072], P(('blk', 'uly')), may hold values from -160 to 160
- keys: bfloat16 [8192, 3072], P(('blk', 'uly')), may hold values from -8 to 8
- values: bfloat16 [8192, 3072], P(('blk', 'uly')), may hold values from -6 to 6
- block_mask: int32 [24, 64, 64], replicated, may hold values from 0 to 1, as said below
- plan: int32 [24], replicated, may hold values from 0 to 23, each once
Outputs:
- attended: bfloat16 [8192, 3072], P(('blk', 'uly'))
The draws below stay inside these ranges and needn't reach their ends.
Inputs may be any that keep to these rules, and one draw needn't show every extreme that they name: `block_mask`: every head's diagonal blocks are 1. Each device along `blk` attends for exactly one block of 128 tokens (block b belongs to blk device b). Cut the heads into 4 groups of 6 consecutive heads; for two different runs and one group, at most 2 pairs of a head and a key block of the second run have a 1 in some query block of the first run, and in every group, for some first run every second run reaches 2.
All inputs are finite; a program needn't handle non-finite values.
Results may differ from the reference program's by a relative error of at most 0.0055.
Values may be sent and summed in bfloat16 or wider, within the bound.
A program may use at most 128 MiB of HBM per device.

```python
import math
import jax
import jax.numpy as jnp
from jax import lax

H = 24
HD = 128
BT = 128
CAP = 2
TOK_DEV = 32
TOKENS = 8192
N_ULY = 4
N_BLK = 64


def shared_normal(key):
    return jax.random.normal(key, (TOKENS, H * HD), jnp.float32)


def draw_keys(key, part):
    base = shared_normal(key)
    return jnp.clip(base, -6.0, 6.0).astype(jnp.bfloat16)


def draw_queries(key, part):
    key = jax.random.fold_in(key, 7)
    own = jax.random.normal(key, (TOKENS, H * HD), jnp.float32)
    return jnp.clip(2.5 * own, -12.0, 12.0).astype(jnp.bfloat16)


def draw_block_mask(key, part):
    key = jax.random.fold_in(key, 3)
    subkeys = jax.random.split(key, 6)
    group = H // N_ULY
    per_dev = TOK_DEV * N_ULY // BT
    units = group * per_dev
    devs = N_BLK
    blocks = devs * per_dev
    counts = jax.random.randint(subkeys[0], (N_ULY, devs, devs), 0, CAP + 1)
    fullest = jax.random.randint(subkeys[1], (N_ULY,), 0, devs)
    receiver = jnp.arange(devs, dtype=jnp.int32)[None, :, None]
    counts = jnp.where(receiver == fullest[:, None, None], CAP, counts)
    scores = jax.random.randint(subkeys[2], (N_ULY, devs, devs, units), 0, 1 << 20) * units + jnp.arange(units, dtype=jnp.int32)
    ranks = jnp.argsort(jnp.argsort(scores, axis=-1), axis=-1)
    chosen = ranks < counts[..., None]
    coin = jax.random.randint(subkeys[3], (N_ULY, devs, devs, units, per_dev), 0, 10) < 7
    forced = jax.random.randint(subkeys[4], (N_ULY, devs, devs, units), 0, per_dev)
    pattern = jnp.logical_or(coin, jnp.arange(per_dev, dtype=jnp.int32) == forced[..., None])
    picked = jnp.logical_and(chosen[..., None], pattern)
    picked = picked.reshape(N_ULY, devs, devs, group, per_dev, per_dev)
    picked = jnp.transpose(picked, (0, 3, 1, 5, 2, 4)).reshape(H, blocks, blocks).astype(jnp.int32)
    owner = jnp.arange(blocks, dtype=jnp.int32) // per_dev
    same = (owner[:, None] == owner[None, :])[None, :, :]
    local_bits = jax.random.randint(subkeys[5], (H, blocks, blocks), 0, 2)
    diagonal = jnp.eye(blocks, dtype=jnp.int32)[None, :, :]
    return jnp.where(same, jnp.maximum(local_bits, diagonal), picked)


def levels(stream_key, dims, pieces, smallest, largest):
    gain = 1.0
    for axis_at, shards_of in pieces:
        draws = jax.random.uniform(jax.random.fold_in(jax.random.fold_in(stream_key, 6), axis_at), (shards_of,), jnp.float32, smallest / len(pieces), largest / len(pieces))
        gain = gain * jnp.repeat(jnp.exp(draws), dims[axis_at] // shards_of).reshape((-1,) + (1,) * (len(dims) - 1 - axis_at))
    return gain


def scatter_about(rng, dims, spread, limit, cuts=(), held_as=jnp.bfloat16):
    loudness = levels(rng, dims, cuts, -0.22, 0.18) if cuts else 1.0
    array = jax.random.normal(rng, dims, jnp.float32) * spread * loudness
    return jnp.minimum(jnp.maximum(array, -limit), limit).astype(held_as)


def setup_inputs(seed: int = 0) -> dict:
    arg_keys = jax.random.split(jax.random.key(seed), 6)
    queries = draw_queries(jax.random.fold_in(arg_keys[5], 71), 0)
    keys = draw_keys(jax.random.fold_in(arg_keys[5], 71), 0)
    values = scatter_about(arg_keys[2], (TOKENS, H * HD), 1.0, 6.0, ((0, 256),))
    block_mask = draw_block_mask(jax.random.fold_in(arg_keys[5], 71), 0)
    plan = jax.random.permutation(arg_keys[4], H).astype(jnp.int32)
    return {"queries": queries, "keys": keys, "values": values, "block_mask": block_mask, "plan": plan}


def reference(queries, keys, values, block_mask, plan):
    heads = plan.shape[0]
    size = queries.shape[1] // heads
    count = queries.shape[0]
    q_all = jnp.transpose(jnp.take(queries.reshape(count, heads, size), plan, axis=1), (1, 0, 2))
    k_all = jnp.transpose(jnp.take(keys.reshape(count, heads, size), plan, axis=1), (1, 0, 2))
    v_all = jnp.transpose(jnp.take(values.reshape(count, heads, size), plan, axis=1), (1, 0, 2))
    masks = jnp.take(block_mask, plan, axis=0)
    scale = 1.0 / math.sqrt(size)
    rows = math.gcd(count, 1024)
    steps = count // rows

    def one_head(items):
        q_head, k_head, v_head, m_head = items

        def one_block(index):
            q_rows = lax.dynamic_slice_in_dim(q_head, index * rows, rows, 0)
            m_rows = lax.dynamic_slice_in_dim(m_head, index * (rows // BT), rows // BT, 0)
            allowed = jnp.repeat(jnp.repeat(m_rows, BT, axis=0), BT, axis=1) > 0
            score = jnp.dot(q_rows, k_head.T, preferred_element_type=jnp.float32) * scale
            score = jnp.where(allowed, score, -jnp.inf)
            top = lax.optimization_barrier(jnp.max(score, axis=1, keepdims=True))
            expo = jnp.exp(score - top)
            total = lax.optimization_barrier(jnp.sum(expo, axis=1, keepdims=True))
            mixed = jnp.dot(expo.astype(jnp.bfloat16), v_head, preferred_element_type=jnp.float32)
            return (mixed / total).astype(jnp.bfloat16)
        blocks = lax.map(one_block, jnp.arange(steps, dtype=jnp.int32))
        return blocks.reshape(count, size)
    result = lax.map(one_head, (q_all, k_all, v_all, masks))
    return jnp.transpose(result, (1, 0, 2)).reshape(count, heads * size)
```

```python
import functools
import math

import jax
import jax.numpy as jnp
from jax import lax
from jax.experimental import pallas as pl
from jax.experimental.pallas import tpu as pltpu
from jax.sharding import PartitionSpec as P

MESH = pl.DeviceIdType.MESH
HD = 128
BT = 128
NU = 4
NX, NY, NZ = 2, 4, 8
NR = NX * NY
HL = 6
HG = 2
NG = HL // HG
TD = BT // NU
HALF = NZ // 2
BIG = 1e30
NT = (((1,), (1,)), ((), ()))


def kernel(
    q_in, k_in, v_in, mask_s, plan_s, out_ref,
    k_st, v_st, q_st, k_buf, v_buf, q_buf, shade, acc, top, tot,
    ob, st, ob_in, st_in, fin, got,
    us, ur, ul, rs, rr, qs, qr, os_, or_, ss, sr, fs, fr,
):
    u = lax.axis_index("uly")
    b = lax.axis_index("blk")
    z = b % NZ
    y = (b // NZ) % NY
    x = b // (NZ * NY)
    scale = 1.0 / math.sqrt(HD)

    def blk_at(xx, yy, zz):
        return {"blk": ((xx % NX) * NY + yy % NY) * NZ + zz % NZ}

    def uly_at(k):
        return {"uly": (u + k) % NU}

    up, down = blk_at(x, y, z + 1), blk_at(x, y, z + NZ - 1)
    plane = [blk_at(x + r // NY, y + r % NY, z) for r in range(NR)]

    barrier = pltpu.get_barrier_semaphore()
    partners = [uly_at(k) for k in range(1, NU)] + [up, down] + plane[1:]
    for device in partners:
        pl.semaphore_signal(barrier, inc=1, device_id=device, device_id_type=MESH)
    pl.semaphore_wait(barrier, len(partners))

    def remote(src, dst, send, recv, device):
        return pltpu.make_async_remote_copy(
            src_ref=src, dst_ref=dst, send_sem=send, recv_sem=recv, device_id=device, device_id_type=MESH
        )

    ins = ((k_in, k_st), (v_in, v_st), (q_in, q_st))

    def own_in(g, a):
        src, dst = ins[a]
        columns = pl.ds(pl.multiple_of((u * HL + g * HG) * HD, HD), HG * HD)
        rows = pl.ds(pl.multiple_of(u * TD, TD), TD)
        return pltpu.make_async_copy(src.at[:, columns], dst.at[g, rows, :], ul.at[g, a])

    def uly_in(g, a, k):
        src, dst = ins[a]
        columns = pl.ds(pl.multiple_of((((u + k) % NU) * HL + g * HG) * HD, HD), HG * HD)
        rows = pl.ds(pl.multiple_of(u * TD, TD), TD)
        return remote(src.at[:, columns], dst.at[g, rows, :], us.at[g, a, k - 1], ur.at[g, a, k - 1], uly_at(k))

    def heads_of(g):
        return pl.ds(g * HG, HG)

    def ring(g, s, i):
        buf = k_buf if i < 2 else v_buf
        right = i % 2 == 0
        src = s - 1 if right else (NZ - s + 1) % NZ
        dst = s if right else NZ - s
        return remote(
            buf.at[src, heads_of(g)], buf.at[dst, heads_of(g)],
            rs.at[g, s - 1, i], rr.at[g, s - 1, i], up if right else down,
        )

    def lanes_of(s):
        return (0, 1, 2, 3) if s < HALF else (0, 3)

    def q_copy(g, j):
        if j == 0:
            src, dst, device = 0, NY, plane[NY]
        else:
            dy = (j - 1) % (NY - 1) + 1
            src = 0 if j < NY else NY
            dst, device = src + dy, blk_at(x, y + NY - dy, z)
        rows = lambda r: q_buf.at[heads_of(g), pl.ds(r * BT, BT), :]
        return remote(rows(src), rows(dst), qs.at[g, j], qr.at[g, j], device)

    def o_copy(g, r):
        return remote(ob.at[g, r], ob_in.at[g, r], os_.at[g, r - 1], or_.at[g, r - 1], plane[r])

    def st_copy(g, r):
        return remote(st.at[g, r], st_in.at[g, r], ss.at[g, r - 1], sr.at[g, r - 1], plane[r])

    def fin_copy(g, k):
        rows = pl.ds(pl.multiple_of(((u + k) % NU) * TD, TD), TD)
        return remote(
            fin.at[heads_of(g), rows, :], got.at[pl.ds(u * HL + g * HG, HG)],
            fs.at[g, k - 1], fr.at[g, k - 1], uly_at(k),
        )

    def arrive(g, a):
        own_in(g, a).wait()
        for k in range(1, NU):
            uly_in(g, a, k).wait_recv()

    def prepare(g):
        arrive(g, 0)
        for hh in range(HG):
            k_buf[0, g * HG + hh] = k_st[g, :, hh * HD:(hh + 1) * HD]
        arrive(g, 1)
        for hh in range(HG):
            v_buf[0, g * HG + hh] = v_st[g, :, hh * HD:(hh + 1) * HD].T
        arrive(g, 2)
        for hh in range(HG):
            q_buf[g * HG + hh, 0:BT, :] = q_st[g, :, hh * HD:(hh + 1) * HD]
        for j in range(NY):
            q_copy(g, j).start()

    def launch(g):
        for i in lanes_of(1):
            ring(g, 1, i).start()

    def relay(g):
        q_copy(g, 0).wait_recv()
        for j in range(NY, 2 * NY - 1):
            q_copy(g, j).start()

    def tick(g, s):
        for i in lanes_of(s):
            ring(g, s, i).wait_recv()
            if s < HALF and i in lanes_of(s + 1):
                ring(g, s + 1, i).start()

    def unit(g, slots, first=False):
        def head(hh, carry):
            h = g * HG + hh
            keys = jnp.concatenate([k_buf[t, h] for t in slots], axis=0)
            vals = jnp.concatenate([v_buf[t, h] for t in slots], axis=1)
            for pair in range(NR // 2):
                lanes = slice(pair * 2 * BT, (pair + 1) * 2 * BT)
                score = lax.dot_general(keys, q_buf[h, lanes, :], NT, preferred_element_type=jnp.float32)
                parts = [score[i * BT:(i + 1) * BT] for i in range(len(slots))]
                shades = [shade[h, t:t + 1, lanes] for t in slots]
                tops = [jnp.minimum(jnp.max(p, axis=0, keepdims=True), -m) for p, m in zip(parts, shades)]
                new_top = functools.reduce(jnp.maximum, tops)
                if not first:
                    old_top = top[h, :, lanes]
                    new_top = jnp.maximum(new_top, old_top)
                    fade = jnp.exp((old_top - new_top) * scale)
                expo = [jnp.exp((p - jnp.maximum(new_top, m)) * scale) for p, m in zip(parts, shades)]
                total = sum(jnp.sum(e, axis=0, keepdims=True) for e in expo)
                weight = jnp.concatenate([e.astype(jnp.bfloat16) for e in expo], axis=0)
                update = jnp.dot(vals, weight, preferred_element_type=jnp.float32)
                if not first:
                    update = update + acc[h, :, lanes] * fade
                    total = total + tot[h, :, lanes] * fade
                acc[h, :, lanes] = update
                tot[h, :, lanes] = total
                top[h, :, lanes] = new_top
            return carry

        lax.fori_loop(0, HG, head, 0)

    def give_back(g):
        for r in range(1, NR):
            lanes = slice(r * BT, (r + 1) * BT)
            for hh in range(HG):
                h = g * HG + hh
                ob[g, r, hh * HD:(hh + 1) * HD, :] = acc[h, :, lanes].astype(jnp.bfloat16)
                st[g, r, 2 * hh:2 * hh + 1, :] = top[h, :, lanes]
                st[g, r, 2 * hh + 1:2 * hh + 2, :] = tot[h, :, lanes]
            st_copy(g, r).start()
            o_copy(g, r).start()

    def combine(g):
        for r in range(1, NR):
            st_copy(g, r).wait_recv()
            o_copy(g, r).wait_recv()
        for hh in range(HG):
            h = g * HG + hh
            tops = [top[h, :, 0:BT]] + [st_in[g, r, 2 * hh:2 * hh + 1, :] for r in range(1, NR)]
            tots = [tot[h, :, 0:BT]] + [st_in[g, r, 2 * hh + 1:2 * hh + 2, :] for r in range(1, NR)]
            best = functools.reduce(jnp.maximum, tops)
            fades = [jnp.exp((t - best) * scale) for t in tops]
            total = sum(f * t for f, t in zip(fades, tots))
            mixed = acc[h, :, 0:BT] * fades[0]
            for r in range(1, NR):
                mixed = mixed + ob_in[g, r, hh * HD:(hh + 1) * HD, :].astype(jnp.float32) * fades[r]
            fin[h] = (mixed / total).T.astype(jnp.bfloat16)
            got[u * HL + h] = fin[h, pl.ds(pl.multiple_of(u * TD, TD), TD), :]
        for k in range(1, NU):
            fin_copy(g, k).start()

    for g in range(NG):
        for a in range(3):
            for k in range(1, NU):
                uly_in(g, a, k).start()
            own_in(g, a).start()

    def shades(h, carry):
        for t in range(NZ):
            for r in range(NR):
                where = ((x + r // NY) % NX) * NY + (y + r % NY) % NY
                allowed = mask_s[h * (NR * NZ) + where * NZ + (z + NZ - t) % NZ]
                value = jnp.where(allowed > 0, -BIG, BIG).astype(jnp.float32)
                shade[h, t:t + 1, r * BT:(r + 1) * BT] = jnp.full((1, BT), value, jnp.float32)
        return carry

    lax.fori_loop(0, HL, shades, 0)
    prepare(0)
    launch(0)

    def group(g, carry):
        tick(g, 1)

        @pl.when(g == 0)
        def _():
            relay(g)

        @pl.when(g + 1 < NG)
        def _():
            prepare(g + 1)

        tick(g, 2)
        for j in range(1, 2 * NY - 1):
            q_copy(g, j).wait_recv()
        unit(g, (0,), first=True)
        unit(g, (1, 7))
        tick(g, 3)

        @pl.when(g + 1 < NG)
        def _():
            launch(g + 1)
            relay(g + 1)

        unit(g, (2, 6))

        @pl.when(g > 0)
        def _():
            combine(g - 1)

        unit(g, (3, 5))
        tick(g, 4)
        unit(g, (4,))
        give_back(g)
        return carry

    lax.fori_loop(0, NG, group, 0)
    combine(NG - 1)
    for g in range(NG):
        for k in range(1, NU):
            fin_copy(g, k).wait_recv()
    for s in range(NU * HL):
        out_ref[:, s * HD:(s + 1) * HD] = got[plan_s[s]]

    def drain(g, carry):
        for a in range(3):
            for k in range(1, NU):
                uly_in(g, a, k).wait_send()
        for s in range(1, HALF + 1):
            for i in lanes_of(s):
                ring(g, s, i).wait_send()
        for j in range(2 * NY - 1):
            q_copy(g, j).wait_send()
        for r in range(1, NR):
            st_copy(g, r).wait_send()
            o_copy(g, r).wait_send()
        for k in range(1, NU):
            fin_copy(g, k).wait_send()
        return carry

    lax.fori_loop(0, NG, drain, 0)


def body(queries, keys, values, block_mask, plan):
    u = lax.axis_index("uly")
    b = lax.axis_index("blk")
    mask = block_mask.reshape(NU * HL, NR, NZ, NR, NZ)
    mask = lax.dynamic_slice(mask, (u * HL, 0, b % NZ, b // NZ, 0), (HL, NR, 1, 1, NZ))
    mask = mask.reshape(HL * NR * NZ)
    bf, f32, dma = jnp.bfloat16, jnp.float32, pltpu.SemaphoreType.DMA
    any_, smem = pl.BlockSpec(memory_space=pl.ANY), pl.BlockSpec(memory_space=pltpu.SMEM)
    return pl.pallas_call(
        kernel,
        out_shape=jax.ShapeDtypeStruct(queries.shape, bf),
        in_specs=[any_, any_, any_, smem, smem],
        out_specs=pl.BlockSpec(memory_space=pltpu.VMEM),
        scratch_shapes=[
            pltpu.VMEM((NG, BT, HG * HD), bf),
            pltpu.VMEM((NG, BT, HG * HD), bf),
            pltpu.VMEM((NG, BT, HG * HD), bf),
            pltpu.VMEM((NZ, HL, BT, HD), bf),
            pltpu.VMEM((NZ, HL, HD, BT), bf),
            pltpu.VMEM((HL, NR * BT, HD), bf),
            pltpu.VMEM((HL, NZ, NR * BT), f32),
            pltpu.VMEM((HL, HD, NR * BT), f32),
            pltpu.VMEM((HL, 1, NR * BT), f32),
            pltpu.VMEM((HL, 1, NR * BT), f32),
            pltpu.VMEM((NG, NR, HG * HD, BT), bf),
            pltpu.VMEM((NG, NR, 8, BT), f32),
            pltpu.VMEM((NG, NR, HG * HD, BT), bf),
            pltpu.VMEM((NG, NR, 8, BT), f32),
            pltpu.VMEM((HL, BT, HD), bf),
            pltpu.VMEM((NU * HL, TD, HD), bf),
            dma((NG, 3, NU - 1)), dma((NG, 3, NU - 1)), dma((NG, 3)),
            dma((NG, HALF, 4)), dma((NG, HALF, 4)),
            dma((NG, 2 * NY - 1)), dma((NG, 2 * NY - 1)),
            dma((NG, NR - 1)), dma((NG, NR - 1)), dma((NG, NR - 1)), dma((NG, NR - 1)),
            dma((NG, NU - 1)), dma((NG, NU - 1)),
        ],
        compiler_params=pltpu.CompilerParams(
            collective_id=0, has_side_effects=True, vmem_limit_bytes=48 * 1024 * 1024
        ),
    )(queries, keys, values, mask, plan)


def solution(mesh):
    placed = (P(("blk", "uly"), None), P(("blk", "uly"), None), P(("blk", "uly"), None), P(), P())
    return jax.shard_map(
        body, mesh=mesh, in_specs=placed, out_specs=P(("blk", "uly"), None), check_vma=False
    )
```

```python
import functools
import math

import jax
import jax.numpy as jnp
from jax import lax
from jax.experimental import pallas as pl
from jax.experimental.pallas import tpu as pltpu
from jax.sharding import PartitionSpec as P

MESH = pl.DeviceIdType.MESH
HD = 128
BT = 128
NU, NX, NY, NZ = 4, 2, 4, 8
NW = NU * NX
NB = NX * NY * NZ
HL = 3
TD = BT // NU
RUN = NX * BT
LANES = NY * RUN
HALF = NZ // 2
BIG = 1e30
NT = (((1,), (1,)), ((), ()))
RATE = math.log2(math.e) / math.sqrt(HD)
BF, F32 = jnp.bfloat16, jnp.float32


def kernel(
    q_in, k_in, v_in, mask_in, plan_s, out_ref,
    k_st, v_st, q_st, m_st, k_buf, v_buf, q_buf, shade, acc, top, tot,
    ob, st, ob_in, st_in, fin, got,
    us, ur, ul, ml, rs, rr, qs, qr, os_, or_, ss, sr, fs, fr,
):
    u = lax.axis_index("uly")
    b = lax.axis_index("blk")
    z = b % NZ
    y = (b // NZ) % NY
    x = b // (NZ * NY)
    w = u * NX + x

    def blk_at(xx, yy, zz):
        return {"blk": (xx * NY + yy % NY) * NZ + zz % NZ}

    def line_at(k):
        there = (w + k) % NW
        return {"uly": there // NX, "blk": ((there % NX) * NY + y) * NZ + z}

    up, down = blk_at(x, y, z + 1), blk_at(x, y, z + NZ - 1)
    side = [blk_at(x, y + dy, z) for dy in range(NY)]

    barrier = pltpu.get_barrier_semaphore()
    partners = [line_at(k) for k in range(1, NW)] + [up, down] + side[1:]
    for device in partners:
        pl.semaphore_signal(barrier, inc=1, device_id=device, device_id_type=MESH)

    mask_copy = pltpu.make_async_copy(mask_in.at[pl.ds(w * HL, HL)], m_st, ml)
    mask_copy.start()
    ins = ((k_in, k_st), (v_in, v_st), (q_in, q_st))
    here = pl.ds(pl.multiple_of(x * BT + u * TD, TD), TD)

    def own_in(a):
        src, dst = ins[a]
        return pltpu.make_async_copy(
            src.at[:, pl.ds(pl.multiple_of(w * HL * HD, HD), HL * HD)], dst.at[here, :], ul.at[a]
        )

    for a in range(3):
        own_in(a).start()
    pl.semaphore_wait(barrier, len(partners))

    def remote(src, dst, send, recv, device):
        return pltpu.make_async_remote_copy(
            src_ref=src, dst_ref=dst, send_sem=send, recv_sem=recv, device_id=device, device_id_type=MESH
        )

    def line_in(a, k):
        src, dst = ins[a]
        columns = pl.ds(pl.multiple_of(((w + k) % NW) * HL * HD, HD), HL * HD)
        return remote(src.at[:, columns], dst.at[here, :], us.at[a, k - 1], ur.at[a, k - 1], line_at(k))

    def ring(s, a, h, d):
        buf = (k_buf, v_buf)[a]
        src = s - 1 if d == 0 else (NZ - s + 1) % NZ
        dst = s if d == 0 else NZ - s
        i = (a * HL + h) * 2 + d
        return remote(
            buf.at[src, h], buf.at[dst, h], rs.at[s - 1, i], rr.at[s - 1, i], up if d == 0 else down
        )

    def q_copy(h, dy):
        return remote(
            q_buf.at[h, 0:RUN, :], q_buf.at[h, dy * RUN:(dy + 1) * RUN, :],
            qs.at[h, dy - 1], qr.at[h, dy - 1], side[NY - dy],
        )

    def o_copy(h, dy):
        return remote(ob.at[h, dy - 1], ob_in.at[h, dy - 1], os_.at[h, dy - 1], or_.at[h, dy - 1], side[dy])

    def st_copy(h, dy):
        return remote(st.at[h, dy - 1], st_in.at[h, dy - 1], ss.at[h, dy - 1], sr.at[h, dy - 1], side[dy])

    def fin_copy(h, k):
        there = (w + k) % NW
        rows = pl.ds(pl.multiple_of((there % NX) * BT + (there // NX) * TD, TD), TD)
        return remote(fin.at[h, rows, :], got.at[w * HL + h], fs.at[h, k - 1], fr.at[h, k - 1], line_at(k))

    def arrive(a):
        own_in(a).wait()
        for k in range(1, NW):
            line_in(a, k).wait_recv()

    def tick(s, a):
        for h in range(HL):
            for d in range(2):
                ring(s, a, h, d).wait_recv()
                last = a == d
                if last:
                    ring(s + 1, a, h, d).start()
                else:
                    @pl.when(s < HALF - 1)
                    def _():
                        ring(s + 1, a, h, d).start()

    def scores(slot, h, lo):
        return lax.dot_general(k_buf[slot, h], q_buf[h, lo:lo + BT, :], NT, preferred_element_type=F32)

    def soften(slot, h, lo, score, first):
        lanes = slice(lo, lo + BT)
        parts = [score[i * BT:(i + 1) * BT] for i in range(NX)]
        shades = [shade[h, slot * NX + i, :, lanes] for i in range(NX)]
        tops = [jnp.minimum(jnp.max(p, axis=0, keepdims=True), -m) for p, m in zip(parts, shades)]
        new_top = functools.reduce(jnp.maximum, tops)
        fade = None
        if not first:
            old_top = top[h, :, lanes]
            new_top = jnp.maximum(new_top, old_top)
            fade = jnp.exp2((old_top - new_top) * RATE)
        expo = [jnp.exp2((p - jnp.maximum(new_top, m)) * RATE) for p, m in zip(parts, shades)]
        top[h, :, lanes] = new_top
        return expo, fade

    def gather(slot, h, lo, expo, fade):
        lanes = slice(lo, lo + BT)
        weight = jnp.concatenate([e.astype(BF) for e in expo], axis=0)
        update = jnp.dot(v_buf[slot, h], weight, preferred_element_type=F32)
        total = sum(jnp.sum(e, axis=0, keepdims=True) for e in expo)
        if fade is not None:
            update = update + acc[h, :, lanes] * fade
            total = total + tot[h, :, lanes] * fade
        acc[h, :, lanes] = update
        tot[h, :, lanes] = total

    def unit(slot, heads, first=False):
        todo = [(h, lo) for h in heads for lo in range(0, LANES, BT)]
        score = scores(slot, *todo[0])
        held = None
        for i, (h, lo) in enumerate(todo):
            later = scores(slot, *todo[i + 1]) if i + 1 < len(todo) else None
            soft = soften(slot, h, lo, score, first)
            if held is not None:
                gather(slot, *todo[i - 1], *held)
            held, score = soft, later
        gather(slot, *todo[-1], *held)

    def give_back(h):
        for dy in range(1, NY):
            lanes = slice(dy * RUN, (dy + 1) * RUN)
            ob[h, dy - 1] = acc[h, :, lanes].astype(BF)
            st[h, dy - 1, 0:1, :] = top[h, :, lanes]
            st[h, dy - 1, 1:2, :] = tot[h, :, lanes]
            o_copy(h, dy).start()
            st_copy(h, dy).start()

    def combine(h):
        for dy in range(1, NY):
            o_copy(h, dy).wait_recv()
            st_copy(h, dy).wait_recv()
        own = slice(0, RUN)
        tops = [top[h, :, own]] + [st_in[h, dy, 0:1, :] for dy in range(NY - 1)]
        tots = [tot[h, :, own]] + [st_in[h, dy, 1:2, :] for dy in range(NY - 1)]
        best = functools.reduce(jnp.maximum, tops)
        fades = [jnp.exp2((t - best) * RATE) for t in tops]
        total = sum(f * t for f, t in zip(fades, tots))
        mixed = acc[h, :, own] * fades[0]
        for dy in range(NY - 1):
            mixed = mixed + ob_in[h, dy].astype(F32) * fades[dy + 1]
        fin[h] = (mixed / total).T.astype(BF)
        for k in range(1, NW):
            fin_copy(h, k).start()
        got[w * HL + h] = fin[h, here, :]

    for a in range(3):
        for k in range(1, NW):
            line_in(a, k).start()

    mask_copy.wait()
    key_row = lax.broadcasted_iota(jnp.int32, (NZ * NX, NB), 0)
    key_col = lax.broadcasted_iota(jnp.int32, (NZ * NX, NB), 1)
    key_block = ((key_row % NX) * NY + y) * NZ + (z + NZ - key_row // NX) % NZ
    pick_key = (key_col == key_block).astype(F32).astype(BF)
    run_row = lax.broadcasted_iota(jnp.int32, (NB, LANES), 0)
    run_col = lax.broadcasted_iota(jnp.int32, (NB, LANES), 1) // BT
    run_block = ((run_col % NX) * NY + (y + run_col // NX) % NY) * NZ + z
    pick_run = (run_row == run_block).astype(F32).astype(BF)
    for h in range(HL):
        allowed = (m_st[h] > 0).astype(F32).astype(BF)
        rows = lax.dot_general(pick_key, allowed, NT, preferred_element_type=F32).astype(BF)
        rows = jnp.dot(rows, pick_run, preferred_element_type=F32)
        rows = jnp.where(rows > 0.5, -BIG, BIG)
        for i in range(NZ * NX):
            shade[h, i] = rows[i:i + 1, :]

    arrive(0)
    for h in range(HL):
        k_buf[0, h] = k_st[:, h * HD:(h + 1) * HD]
        for d in range(2):
            ring(1, 0, h, d).start()
    arrive(1)
    for h in range(HL):
        v_buf[0, h] = v_st[:, h * HD:(h + 1) * HD].T
        for d in range(2):
            ring(1, 1, h, d).start()
    arrive(2)
    for h in range(HL):
        q_buf[h, 0:RUN, :] = q_st[:, h * HD:(h + 1) * HD]
        for dy in range(1, NY):
            q_copy(h, dy).start()

    heads = range(HL)

    def step(s, carry):
        tick(s, 0)

        @pl.when(s > 1)
        def _():
            unit(NZ + 1 - s, heads)

        tick(s, 1)

        @pl.when(s == 1)
        def _():
            for h in heads:
                for dy in range(1, NY):
                    q_copy(h, dy).wait_recv()
            unit(0, heads, first=True)

        unit(s, heads)
        return carry

    lax.fori_loop(1, HALF, step, 0)
    unit(HALF + 1, heads)
    for h in heads:
        ring(HALF, 0, h, 0).wait_recv()
        ring(HALF, 1, h, 1).wait_recv()
        unit(HALF, [h])
        give_back(h)

    def drain(s, carry):
        for a in range(2):
            for h in heads:
                for d in range(2):
                    ring(s, a, h, d).wait_send()
        return carry

    lax.fori_loop(1, HALF, drain, 0)
    for h in heads:
        ring(HALF, 0, h, 0).wait_send()
        ring(HALF, 1, h, 1).wait_send()
        for dy in range(1, NY):
            q_copy(h, dy).wait_send()
    for a in range(3):
        for k in range(1, NW):
            line_in(a, k).wait_send()
    for h in heads:
        combine(h)
    for h in heads:
        for dy in range(1, NY):
            o_copy(h, dy).wait_send()
            st_copy(h, dy).wait_send()
    for h in heads:
        for k in range(1, NW):
            fin_copy(h, k).wait_recv()
    for s in range(NW * HL):
        out_ref[:, s * HD:(s + 1) * HD] = got[plan_s[s]]
    for h in heads:
        for k in range(1, NW):
            fin_copy(h, k).wait_send()


def body(queries, keys, values, block_mask, plan):
    dma = pltpu.SemaphoreType.DMA
    hbm, smem = pl.BlockSpec(memory_space=pltpu.HBM), pl.BlockSpec(memory_space=pltpu.SMEM)
    return pl.pallas_call(
        kernel,
        out_shape=jax.ShapeDtypeStruct(queries.shape, BF),
        in_specs=[hbm, hbm, hbm, hbm, smem],
        out_specs=pl.BlockSpec(memory_space=pltpu.VMEM),
        scratch_shapes=[
            pltpu.VMEM((RUN, HL * HD), BF),
            pltpu.VMEM((RUN, HL * HD), BF),
            pltpu.VMEM((RUN, HL * HD), BF),
            pltpu.VMEM((HL, NB, NB), jnp.int32),
            pltpu.VMEM((NZ, HL, RUN, HD), BF),
            pltpu.VMEM((NZ, HL, HD, RUN), BF),
            pltpu.VMEM((HL, LANES, HD), BF),
            pltpu.VMEM((HL, NZ * NX, 1, LANES), F32),
            pltpu.VMEM((HL, HD, LANES), F32),
            pltpu.VMEM((HL, 1, LANES), F32),
            pltpu.VMEM((HL, 1, LANES), F32),
            pltpu.VMEM((HL, NY - 1, HD, RUN), BF),
            pltpu.VMEM((HL, NY - 1, 8, RUN), F32),
            pltpu.VMEM((HL, NY - 1, HD, RUN), BF),
            pltpu.VMEM((HL, NY - 1, 8, RUN), F32),
            pltpu.VMEM((HL, RUN, HD), BF),
            pltpu.VMEM((NW * HL, TD, HD), BF),
            dma((3, NW - 1)), dma((3, NW - 1)), dma((3,)), dma,
            dma((HALF, 4 * HL)), dma((HALF, 4 * HL)),
            dma((HL, NY - 1)), dma((HL, NY - 1)),
            dma((HL, NY - 1)), dma((HL, NY - 1)), dma((HL, NY - 1)), dma((HL, NY - 1)),
            dma((HL, NW - 1)), dma((HL, NW - 1)),
        ],
        compiler_params=pltpu.CompilerParams(
            collective_id=0, has_side_effects=True, vmem_limit_bytes=48 * 1024 * 1024
        ),
    )(queries, keys, values, block_mask, plan)


def solution(mesh):
    placed = (P(("blk", "uly"), None), P(("blk", "uly"), None), P(("blk", "uly"), None), P(), P())
    return jax.shard_map(
        body, mesh=mesh, in_specs=placed, out_specs=P(("blk", "uly"), None), check_vma=False
    )
```

```python
import functools
import math

import jax
import jax.numpy as jnp
from jax import lax
from jax.experimental import pallas as pl
from jax.experimental.pallas import tpu as pltpu
from jax.sharding import PartitionSpec as P

MESH = pl.DeviceIdType.MESH
HD = 128
BT = 128
NU, NX, NY, NZ = 4, 2, 4, 8
NW = NU * NX
NB = NX * NY * NZ
HL = 3
TD = BT // NU
RUN = NX * BT
LANES = NY * RUN
HALF = NZ // 2
BIG = 1e30
VMEM_MIB = 62
NT = (((1,), (1,)), ((), ()))
RATE = math.log2(math.e) / math.sqrt(HD)
BF, F32 = jnp.bfloat16, jnp.float32


def kernel(
    q_in, k_in, v_in, mask_in, plan_s, out_ref,
    kv, v_st, q_buf, m_st, shade, acc, top, tot, ob, ob_in, fin, got,
    us, ur, ul, ml, rs, rr, qs, qr, os_, or_, fs, fr,
):
    u = lax.axis_index("uly")
    b = lax.axis_index("blk")
    z = b % NZ
    y = (b // NZ) % NY
    x = b // (NZ * NY)
    w = u * NX + x
    heads = range(HL)

    def blk_at(yy, zz):
        return {"blk": (x * NY + yy % NY) * NZ + zz % NZ}

    def line_at(k):
        there = (w + k) % NW
        return {"uly": there // NX, "blk": ((there % NX) * NY + y) * NZ + z}

    up, down = blk_at(y, z + 1), blk_at(y, z + NZ - 1)
    side = [blk_at(y + dy, z) for dy in range(NY)]

    barrier = pltpu.get_barrier_semaphore()
    partners = [line_at(k) for k in range(1, NW)] + [up, down] + side[1:]
    for device in partners:
        pl.semaphore_signal(barrier, inc=1, device_id=device, device_id_type=MESH)

    mask_copy = pltpu.make_async_copy(mask_in.at[pl.ds(w * HL, HL)], m_st, ml)
    mask_copy.start()
    ins = ((k_in, kv.at[0]), (v_in, v_st), (q_in, q_buf))
    here = pl.ds(pl.multiple_of(x * BT + u * TD, TD), TD)

    def columns_of(there, h):
        return pl.ds(pl.multiple_of((there * HL + h) * HD, HD), HD)

    def own_in(a, h):
        src, dst = ins[a]
        return pltpu.make_async_copy(src.at[:, columns_of(w, h)], dst.at[h, here, :], ul.at[a, h])

    for a in range(3):
        for h in heads:
            own_in(a, h).start()
    pl.semaphore_wait(barrier, len(partners))

    def remote(src, dst, send, recv, device):
        return pltpu.make_async_remote_copy(
            src_ref=src, dst_ref=dst, send_sem=send, recv_sem=recv, device_id=device, device_id_type=MESH
        )

    def sum_of(ref, send, recv):
        return remote(ref, ref, send, recv, up)

    def line_in(a, h, k):
        src, dst = ins[a]
        return remote(
            src.at[:, columns_of((w + k) % NW, h)], dst.at[h, here, :], us.at[a, h], ur.at[a, h], line_at(k)
        )

    def line_all(a, h):
        return sum_of(v_st.at[h, 0:(NW - 1) * TD, :], us.at[a, h], ur.at[a, h])

    def ring(s, h, d):
        src = s - 1 if d == 0 else (NZ - s + 1) % NZ
        dst = s if d == 0 else NZ - s
        return remote(
            kv.at[src, h], kv.at[dst, h], rs.at[s - 1], rr.at[s - 1, h, d], up if d == 0 else down
        )

    def ring_last(h, d):
        rows = slice(d * RUN, (d + 1) * RUN)
        src = HALF - 1 if d == 0 else HALF + 1
        return remote(
            kv.at[src, h, rows, :], kv.at[HALF, h, rows, :],
            rs.at[HALF - 1], rr.at[HALF - 1, h, d], up if d == 0 else down,
        )

    def q_copy(h, dy):
        return remote(
            q_buf.at[h, 0:RUN, :], q_buf.at[h, dy * RUN:(dy + 1) * RUN, :], qs.at[h], qr.at[h], side[NY - dy]
        )

    def q_all(h):
        return sum_of(q_buf.at[h, RUN:NY * RUN, :], qs.at[h], qr.at[h])

    def o_copy(h, dy):
        return remote(ob.at[h, dy - 1], ob_in.at[h, dy - 1], os_.at[h], or_.at[h], side[dy])

    def o_all(h):
        return sum_of(ob_in.at[h], os_.at[h], or_.at[h])

    def fin_copy(h, k):
        there = (w + k) % NW
        rows = pl.ds(pl.multiple_of((there % NX) * BT + (there // NX) * TD, TD), TD)
        return remote(fin.at[h, rows, :], got.at[w * HL + h], fs.at[h], fr.at[h], line_at(k))

    def fin_all(h):
        return sum_of(got.at[0:NW - 1], fs.at[h], fr.at[h])

    def arrive(a, h):
        own_in(a, h).wait()
        line_all(a, h).wait_recv()

    def scores(slot, h, lo):
        return lax.dot_general(kv[slot, h, 0:RUN, :], q_buf[h, lo:lo + BT, :], NT, preferred_element_type=F32)

    def soften(slot, h, lo, score, first):
        lanes = slice(lo, lo + BT)
        parts = [score[i * BT:(i + 1) * BT] for i in range(NX)]
        shades = [shade[h, slot * NX + i, :, lanes] for i in range(NX)]
        tops = [jnp.minimum(jnp.max(p, axis=0, keepdims=True), -m) for p, m in zip(parts, shades)]
        new_top = functools.reduce(jnp.maximum, tops)
        fade = None
        if not first:
            old_top = top[h, :, lanes]
            new_top = jnp.maximum(new_top, old_top)
            fade = jnp.exp2((old_top - new_top) * RATE)
        expo = [jnp.exp2((p - jnp.maximum(new_top, m)) * RATE) for p, m in zip(parts, shades)]
        top[h, :, lanes] = new_top
        return expo, fade

    def gather(slot, h, lo, expo, fade):
        lanes = slice(lo, lo + BT)
        vals = jnp.concatenate([kv[slot, h, RUN + i * BT:RUN + (i + 1) * BT, :] for i in range(NX)], axis=1)
        weight = jnp.concatenate([e.astype(BF) for e in expo], axis=0)
        update = jnp.dot(vals, weight, preferred_element_type=F32)
        total = sum(jnp.sum(e, axis=0, keepdims=True) for e in expo)
        if fade is not None:
            update = update + acc[h, :, lanes] * fade
            total = total + tot[h, :, lanes] * fade
        acc[h, :, lanes] = update
        tot[h, :, lanes] = total

    def unit(pairs, first=False):
        todo = [(slot, h, lo) for slot, h in pairs for lo in range(0, LANES, BT)]
        score = scores(*todo[0])
        held = None
        for i, item in enumerate(todo):
            later = scores(*todo[i + 1]) if i + 1 < len(todo) else None
            soft = soften(*item, score, first)
            if held is not None:
                gather(*todo[i - 1], *held)
            held, score = soft, later
        gather(*todo[-1], *held)

    def split3(value):
        terms = []
        for _ in range(3):
            term = value.astype(BF).astype(F32)
            terms.append(term)
            value = value - term
        return terms

    def give_back(h):
        row = lax.broadcasted_iota(jnp.int32, (16, RUN), 0)
        for dy in range(1, NY):
            lanes = slice(dy * RUN, (dy + 1) * RUN)
            ob[h, dy - 1, 0:HD, :] = acc[h, :, lanes].astype(BF)
            notes = jnp.zeros((16, RUN), F32)
            for i, term in enumerate(split3(top[h, :, lanes]) + split3(tot[h, :, lanes])):
                notes = jnp.where(row == i, term, notes)
            ob[h, dy - 1, HD:HD + 16, :] = notes.astype(BF)
            o_copy(h, dy).start()

    def combine(h):
        o_all(h).wait_recv()
        own = slice(0, RUN)
        notes = [ob_in[h, dy, HD:HD + 16, :].astype(F32) for dy in range(NY - 1)]
        tops = [top[h, :, own]] + [n[0:1] + n[1:2] + n[2:3] for n in notes]
        tots = [tot[h, :, own]] + [n[3:4] + n[4:5] + n[5:6] for n in notes]
        best = functools.reduce(jnp.maximum, tops)
        fades = [jnp.exp2((t - best) * RATE) for t in tops]
        share = 1.0 / sum(f * t for f, t in zip(fades, tots))
        mixed = acc[h, :, own] * (fades[0] * share)
        for dy in range(NY - 1):
            mixed = mixed + ob_in[h, dy, 0:HD, :].astype(F32) * (fades[dy + 1] * share)
        fin[h] = mixed.astype(BF).T
        for k in range(1, NW):
            fin_copy(h, k).start()
        got[w * HL + h] = fin[h, here, :]

    for h in heads:
        for a in range(2):
            for k in range(1, NW):
                line_in(a, h, k).start()
    for h in heads:
        for k in range(1, NW):
            line_in(2, h, k).start()

    for h in heads:
        arrive(0, h)
        arrive(1, h)
        for i in range(NX):
            kv[0, h, RUN + i * BT:RUN + (i + 1) * BT, :] = v_st[h, i * BT:(i + 1) * BT, :].T
        for d in range(2):
            ring(1, h, d).start()
    for h in heads:
        arrive(2, h)
        for dy in range(1, NY):
            q_copy(h, dy).start()

    mask_copy.wait()
    key_row = lax.broadcasted_iota(jnp.int32, (NZ * NX, NB), 0)
    key_col = lax.broadcasted_iota(jnp.int32, (NZ * NX, NB), 1)
    key_block = ((key_row % NX) * NY + y) * NZ + (z + NZ - key_row // NX) % NZ
    pick_key = (key_col == key_block).astype(F32).astype(BF)
    run_row = lax.broadcasted_iota(jnp.int32, (NB, LANES), 0)
    run_col = lax.broadcasted_iota(jnp.int32, (NB, LANES), 1) // BT
    run_block = ((run_col % NX) * NY + (y + run_col // NX) % NY) * NZ + z
    pick_run = (run_row == run_block).astype(F32).astype(BF)
    for h in heads:
        allowed = (m_st[h] > 0).astype(F32).astype(BF)
        rows = lax.dot_general(pick_key, allowed, NT, preferred_element_type=F32).astype(BF)
        rows = jnp.dot(rows, pick_run, preferred_element_type=F32)
        rows = jnp.where(rows > 0.5, -BIG, BIG)
        for i in range(NZ * NX):
            shade[h, i] = rows[i:i + 1, :]

    def tick(s, h):
        ring(s, h, 0).wait_recv()
        ring(s, h, 1).wait_recv()

    def forward(s, h):
        ring(s, h, 0).start()
        ring(s, h, 1).start()

    def step(s, carry):
        tick(s, 0)
        forward(s + 1, 0)

        @pl.when(s > 1)
        def _():
            unit([(s - 1, h) for h in heads])

        tick(s, 1)
        forward(s + 1, 1)

        @pl.when(s > 1)
        def _():
            unit([(NZ + 1 - s, h) for h in heads])

        tick(s, 2)

        @pl.when(s == 1)
        def _():
            forward(s + 1, 2)
            for h in heads:
                q_all(h).wait_recv()
            unit([(0, h) for h in heads], first=True)

        return carry

    lax.fori_loop(1, HALF - 1, step, 0)

    def finish(h):
        unit([(HALF - 1, h), (HALF + 1, h)])
        for d in range(2):
            ring_last(h, d).wait_recv()
        unit([(HALF, h)])
        give_back(h)

    def last(h):
        for d in range(2):
            ring_last(h, d).start()

    tick(HALF - 1, 0)
    last(0)
    forward(HALF - 1, 2)
    unit([(HALF - 2, h) for h in heads])
    tick(HALF - 1, 1)
    last(1)
    unit([(HALF + 2, h) for h in heads])
    finish(0)
    tick(HALF - 1, 2)
    last(2)
    finish(1)
    combine(0)
    finish(2)
    for s in range(1, HALF):
        sum_of(kv.at[0:2], rs.at[s - 1], rr.at[s - 1, 0, 0]).wait_send()
    sum_of(kv.at[0], rs.at[HALF - 1], rr.at[HALF - 1, 0, 0]).wait_send()
    for h in heads:
        q_all(h).wait_send()
        for a in range(3):
            line_all(a, h).wait_send()
    combine(1)
    combine(2)
    for h in heads:
        o_all(h).wait_send()
    for h in heads:
        fin_all(h).wait_recv()
    for s in range(NW * HL):
        out_ref[:, s * HD:(s + 1) * HD] = got[plan_s[s]]
    for h in heads:
        fin_all(h).wait_send()


def body(queries, keys, values, block_mask, plan):
    dma = pltpu.SemaphoreType.DMA
    hbm, smem = pl.BlockSpec(memory_space=pl.ANY), pl.BlockSpec(memory_space=pltpu.SMEM)
    return pl.pallas_call(
        kernel,
        out_shape=jax.ShapeDtypeStruct(queries.shape, BF),
        in_specs=[hbm, hbm, hbm, hbm, smem],
        out_specs=pl.BlockSpec(memory_space=pltpu.VMEM),
        scratch_shapes=[
            pltpu.VMEM((NZ, HL, 2 * RUN, HD), BF),
            pltpu.VMEM((HL, RUN, HD), BF),
            pltpu.VMEM((HL, LANES, HD), BF),
            pltpu.VMEM((HL, NB, NB), jnp.int32),
            pltpu.VMEM((HL, NZ * NX, 1, LANES), F32),
            pltpu.VMEM((HL, HD, LANES), F32),
            pltpu.VMEM((HL, 1, LANES), F32),
            pltpu.VMEM((HL, 1, LANES), F32),
            pltpu.VMEM((HL, NY - 1, HD + 16, RUN), BF),
            pltpu.VMEM((HL, NY - 1, HD + 16, RUN), BF),
            pltpu.VMEM((HL, RUN, HD), BF),
            pltpu.VMEM((NW * HL, TD, HD), BF),
            dma((3, HL)), dma((3, HL)), dma((3, HL)), dma,
            dma((HALF,)), dma((HALF, HL, 2)),
            dma((HL,)), dma((HL,)),
            dma((HL,)), dma((HL,)),
            dma((HL,)), dma((HL,)),
        ],
        compiler_params=pltpu.CompilerParams(
            collective_id=0, has_side_effects=True, vmem_limit_bytes=VMEM_MIB * 1024 * 1024
        ),
    )(queries, keys, values, block_mask, plan)


def solution(mesh):
    placed = (P(("blk", "uly"), None), P(("blk", "uly"), None), P(("blk", "uly"), None), P(), P())
    return jax.shard_map(
        body, mesh=mesh, in_specs=placed, out_specs=P(("blk", "uly"), None), check_vma=False
    )
```

```python
import functools
import math

import jax
import jax.numpy as jnp
from jax import lax
from jax.experimental import pallas as pl
from jax.experimental.pallas import tpu as pltpu
from jax.sharding import PartitionSpec as P

MESH = pl.DeviceIdType.MESH
H, HD, BT, TD = 24, 128, 128, 32
NX, NY, NZ = 4, 4, 8
NB = 64
HL = H // NZ
SETS = 3
RUN = NZ * TD
LANES = NX * RUN
BIG, FLOOR = 1e30, -1e29
VMEM_MIB = 62
NT = (((1,), (1,)), ((), ()))
RATE = math.log2(math.e) / math.sqrt(HD)
BF, F32 = jnp.bfloat16, jnp.float32
K, V, Q = 0, 1, 2


def kernel(
    q_in, k_in, v_in, mask_in, plan_s, out_ref,
    kb, vb, v_st, q_buf, m_st, shade, acc, top, tot, ob, ob_in, fin, got,
    us, ur, ul, ml, ys, yr, cs, cr, qs, qr, os_, or_, fs, fr,
):
    u = lax.axis_index("uly")
    b = lax.axis_index("blk")
    core = u % 2
    z = b % NZ
    y = (b // NZ) % NY
    x = (u // 2) * 2 + b // (NZ * NY)

    def at(xx, yy, zz, cc):
        xx, yy, zz = xx % NX, yy % NY, zz % NZ
        return {"uly": (xx // 2) * 2 + cc, "blk": ((xx % 2) * NY + yy) * NZ + zz}

    same = [at(x, y, z + k, core) for k in range(NZ)]
    cross = [at(x, y, z + k, 1 - core) for k in range(NZ)]
    y_side = [at(x, y + d, z, core) for d in range(NY)]
    x_side = [at(x + d, y, z, core) for d in range(NX)]

    barrier = pltpu.get_barrier_semaphore()
    partners = same[1:] + cross + y_side[1:] + x_side[1:]
    for device in partners:
        pl.semaphore_signal(barrier, inc=1, device_id=device, device_id_type=MESH)

    mask_copy = pltpu.make_async_copy(mask_in.at[pl.ds(z * HL, HL)], m_st, ml)
    mask_copy.start()
    here = pl.ds(pl.multiple_of(z * TD, TD), TD)
    sources = (k_in, v_in, q_in)

    def place(a, i):
        if a == V:
            return v_st.at[i, here, :]
        if a == Q:
            return q_buf.at[i, here, :]
        return kb.at[i // 2, 0, i % 2, here, :]

    def columns_of(i, k):
        there = (z + k) % NZ
        lead = (2 * core, 2 - 2 * core, 1)[i]
        return pl.ds(pl.multiple_of((there * HL + lead) * HD, HD), HD)

    def own_in(a, i):
        return pltpu.make_async_copy(sources[a].at[:, columns_of(i, 0)], place(a, i), ul.at[a, i])

    for a in range(3):
        for i in (2, 0):
            own_in(a, i).start()
    pl.semaphore_wait(barrier, len(partners))

    def remote(src, dst, send, recv, device):
        return pltpu.make_async_remote_copy(
            src_ref=src, dst_ref=dst, send_sem=send, recv_sem=recv, device_id=device, device_id_type=MESH
        )

    def sum_of(ref, send, recv):
        return remote(ref, ref, send, recv, same[1])

    def first_of(i):
        return 0 if i == 1 else 1

    def entry(a, i, k):
        device = cross[k] if i == 1 else same[k]
        return remote(sources[a].at[:, columns_of(i, k)], place(a, i), us.at[a, i], ur.at[a, i], device)

    def entry_all(a, i):
        return sum_of(v_st.at[i, 0:(NZ - first_of(i)) * TD, :], us.at[a, i], ur.at[a, i])

    def send_in(a, i):
        for k in range(first_of(i), NZ):
            entry(a, i, k).start()

    def arrive(a, i):
        if i != 1:
            own_in(a, i).wait()
        entry_all(a, i).wait_recv()

    def y_copy(hk, a, d):
        buf = vb if a == V else kb
        src, dst = (buf.at[0, 0], buf.at[0, d]) if hk == 0 else (buf.at[1, 0, 0], buf.at[1, d, 0])
        return remote(src, dst, ys.at[hk, a], yr.at[hk, a, d - 1], y_side[NY - d])

    def y_all(hk, a):
        ref = kb.at[0, 1:NY] if hk == 0 else kb.at[1, 1:NY, 0]
        return sum_of(ref, ys.at[hk, a], yr.at[hk, a, 0])

    def c_copy(a, d):
        buf = vb if a == V else kb
        return remote(buf.at[1, d, 0], buf.at[1, d, 1], cs.at[a], cr.at[a, d], cross[0])

    def c_all(a):
        return sum_of(kb.at[1, 0:NY, 0], cs.at[a], cr.at[a, 0])

    def q_copy(i, d):
        return remote(
            q_buf.at[i, 0:RUN, :], q_buf.at[i, d * RUN:(d + 1) * RUN, :], qs.at[i], qr.at[i], x_side[NX - d]
        )

    def q_all(i):
        return sum_of(q_buf.at[i, RUN:LANES, :], qs.at[i], qr.at[i])

    def o_copy(i, d):
        return remote(ob.at[i, d - 1], ob_in.at[i, d - 1], os_.at[i], or_.at[i], x_side[d])

    def o_all(i):
        return sum_of(ob_in.at[i], os_.at[i], or_.at[i])

    mine = (z * HL + 2 * core, z * HL + 2 * core, z * HL + 1)

    def fin_copy(i, k):
        rows = pl.ds(pl.multiple_of(((z + k) % NZ) * TD, TD), TD)
        device = cross[k] if i == 1 else same[k]
        return remote(fin.at[i, rows, :], got.at[mine[i]], fs.at[i], fr.at[i], device)

    def fin_all(i):
        return sum_of(got.at[0:NZ - first_of(i)], fs.at[i], fr.at[i])

    def turn(i):
        for n in range(RUN // HD):
            rows = slice(n * HD, (n + 1) * HD)
            vb[i // 2, 0, i % 2, rows, :] = v_st[i, rows, :].T

    def scores(d, half, i, lo):
        return lax.dot_general(kb[i // 2, d, half], q_buf[i, lo:lo + BT, :], NT, preferred_element_type=F32)

    def soften(d, half, i, lo, score, first):
        lanes = slice(lo, lo + BT)
        bias = shade[i // 2, d, :, lanes]
        parts = [score[n * TD:(n + 1) * TD] for n in range(NZ)]
        tops = [jnp.max(p.reshape(TD // 8, 8, BT), axis=0) + bias[n:n + 1] for n, p in enumerate(parts)]
        new_top = jnp.maximum(jnp.max(functools.reduce(jnp.maximum, tops), axis=0, keepdims=True), FLOOR)
        fade = None
        if not first:
            old_top = top[i, :, lanes]
            new_top = jnp.maximum(new_top, old_top)
            fade = jnp.exp2((old_top - new_top) * RATE)
        shift = (bias - new_top) * RATE
        expo = [jnp.exp2(p * RATE + shift[n:n + 1]) for n, p in enumerate(parts)]
        top[i, :, lanes] = new_top
        return jnp.concatenate(expo, axis=0), fade

    def gather(d, half, i, lo, expo, fade):
        lanes = slice(lo, lo + BT)
        vals = jnp.concatenate([vb[i // 2, d, half, n * HD:(n + 1) * HD, :] for n in range(RUN // HD)], axis=1)
        update = jnp.dot(vals, expo.astype(BF), preferred_element_type=F32)
        total = jnp.sum(expo, axis=0, keepdims=True)
        if fade is not None:
            update = update + acc[i, :, lanes] * fade
            total = total + tot[i, :, lanes] * fade
        acc[i, :, lanes] = update
        tot[i, :, lanes] = total

    def unit(parts, first=False):
        todo = [(d, half, i, lo) for d, half, i in parts for lo in range(0, LANES, BT)]
        fresh = len(parts) if first is True else first
        score = scores(*todo[0])
        held = None
        for n, item in enumerate(todo):
            later = scores(*todo[n + 1]) if n + 1 < len(todo) else None
            soft = soften(*item, score, n < fresh * (LANES // BT))
            if held is not None:
                gather(*todo[n - 1], *held)
            held, score = soft, later
        gather(*todo[-1], *held)

    def split3(value):
        terms = []
        for _ in range(3):
            term = value.astype(BF).astype(F32)
            terms.append(term)
            value = value - term
        return terms

    def give_back(i):
        row = lax.broadcasted_iota(jnp.int32, (16, RUN), 0)
        for d in range(1, NX):
            lanes = slice(d * RUN, (d + 1) * RUN)
            ob[i, d - 1, 0:HD, :] = acc[i, :, lanes].astype(BF)
            notes = jnp.zeros((16, RUN), F32)
            for n, term in enumerate(split3(top[i, :, lanes]) + split3(tot[i, :, lanes])):
                notes = jnp.where(row == n, term, notes)
            ob[i, d - 1, HD:HD + 16, :] = notes.astype(BF)
            o_copy(i, d).start()

    def combine(i):
        o_all(i).wait_recv()
        own = slice(0, RUN)
        notes = [ob_in[i, d, HD:HD + 16, :].astype(F32) for d in range(NX - 1)]
        tops = [top[i, :, own]] + [n[0:1] + n[1:2] + n[2:3] for n in notes]
        tots = [tot[i, :, own]] + [n[3:4] + n[4:5] + n[5:6] for n in notes]
        best = functools.reduce(jnp.maximum, tops)
        fades = [jnp.exp2((t - best) * RATE) for t in tops]
        share = 1.0 / sum(f * t for f, t in zip(fades, tots))
        mixed = acc[i, :, own] * (fades[0] * share)
        for d in range(NX - 1):
            mixed = mixed + ob_in[i, d, 0:HD, :].astype(F32) * (fades[d + 1] * share)
        fin[i] = mixed.astype(BF).T
        for k in range(first_of(i), NZ):
            fin_copy(i, k).start()
        if i != 1:
            got[mine[i]] = fin[i, here, :]

    for a in (K, V, Q):
        send_in(a, 2)
    for a in (K, Q, V):
        send_in(a, 0)
        send_in(a, 1)

    arrive(K, 2)
    for d in range(1, NY):
        y_copy(1, K, d).start()
    c_copy(K, 0).start()
    arrive(V, 2)
    turn(2)
    for d in range(1, NY):
        y_copy(1, V, d).start()
    c_copy(V, 0).start()
    arrive(Q, 2)
    for d in range(1, NX):
        q_copy(2, d).start()

    mask_copy.wait()
    key_row = lax.broadcasted_iota(jnp.int32, (NY * NZ, NB), 0)
    key_col = lax.broadcasted_iota(jnp.int32, (NY * NZ, NB), 1)
    key_block = ((x % 2) * NY + (y + key_row // NZ) % NY) * NZ + key_row % NZ
    pick_key = (key_col == key_block).astype(F32).astype(BF)
    run_row = lax.broadcasted_iota(jnp.int32, (NB, LANES), 0)
    run_col = lax.broadcasted_iota(jnp.int32, (NB, LANES), 1)
    run_block = (((x + run_col // RUN) % 2) * NY + y) * NZ + (run_col // TD) % NZ
    pick_run = (run_row == run_block).astype(F32).astype(BF)
    for hk in range(2):
        allowed = (m_st[2 * core if hk == 0 else 1] > 0).astype(F32).astype(BF)
        rows = lax.dot_general(pick_key, allowed, NT, preferred_element_type=F32).astype(BF)
        rows = jnp.dot(rows, pick_run, preferred_element_type=F32)
        rows = jnp.where(rows > 0.5, 0.0, -BIG)
        for d in range(NY):
            shade[hk, d] = rows[d * NZ:(d + 1) * NZ, :]

    for i in (0, 1):
        arrive(K, i)
    for d in range(1, NY):
        y_copy(0, K, d).start()
    for i in (0, 1):
        arrive(Q, i)
        for d in range(1, NX):
            q_copy(i, d).start()
    for i in (0, 1):
        arrive(V, i)
        turn(i)
    for d in range(1, NY):
        y_copy(0, V, d).start()

    for d in (1, 3, 2):
        for a in (K, V):
            y_copy(1, a, d).wait_recv()
            c_copy(a, d).start()
    q_all(2).wait_recv()
    unit([(d, 0, 2) for d in (0, 1, 3, 2)], first=1)
    for d in range(NY):
        for a in (K, V):
            c_copy(a, d).wait_recv()
    unit([(d, 1, 2) for d in range(NY)])
    give_back(2)
    for i in (0, 1):
        q_all(i).wait_recv()
        unit([(0, 0, i), (0, 1, i)], first=1)
    for d in (1, 3):
        for a in (K, V):
            y_copy(0, a, d).wait_recv()
        unit([(d, half, i) for i in (0, 1) for half in (0, 1)])
    combine(2)
    for a in (K, V):
        y_copy(0, a, 2).wait_recv()
    for i in (0, 1):
        unit([(2, 0, i), (2, 1, i)])
        give_back(i)

    for i in range(SETS):
        for a in range(3):
            entry_all(a, i).wait_send()
        q_all(i).wait_send()
    for a in (K, V):
        y_all(0, a).wait_send()
        y_all(1, a).wait_send()
        c_all(a).wait_send()
    combine(0)
    combine(1)
    for i in range(SETS):
        o_all(i).wait_send()
    for i in (2, 0, 1):
        fin_all(i).wait_recv()
    for s in range(H):
        out_ref[:, s * HD:(s + 1) * HD] = got[plan_s[s]]
    for i in range(SETS):
        fin_all(i).wait_send()


def body(queries, keys, values, block_mask, plan):
    dma = pltpu.SemaphoreType.DMA
    hbm, smem = pl.BlockSpec(memory_space=pl.ANY), pl.BlockSpec(memory_space=pltpu.SMEM)
    return pl.pallas_call(
        kernel,
        out_shape=jax.ShapeDtypeStruct(queries.shape, BF),
        in_specs=[hbm, hbm, hbm, hbm, smem],
        out_specs=pl.BlockSpec(memory_space=pltpu.VMEM),
        scratch_shapes=[
            pltpu.VMEM((2, NY, 2, RUN, HD), BF),
            pltpu.VMEM((2, NY, 2, RUN, HD), BF),
            pltpu.VMEM((SETS, RUN, HD), BF),
            pltpu.VMEM((SETS, LANES, HD), BF),
            pltpu.VMEM((HL, NB, NB), jnp.int32),
            pltpu.VMEM((2, NY, NZ, LANES), F32),
            pltpu.VMEM((SETS, HD, LANES), F32),
            pltpu.VMEM((SETS, 1, LANES), F32),
            pltpu.VMEM((SETS, 1, LANES), F32),
            pltpu.VMEM((SETS, NX - 1, HD + 16, RUN), BF),
            pltpu.VMEM((SETS, NX - 1, HD + 16, RUN), BF),
            pltpu.VMEM((SETS, RUN, HD), BF),
            pltpu.VMEM((H, TD, HD), BF),
            dma((3, SETS)), dma((3, SETS)), dma((3, SETS)), dma,
            dma((2, 2)), dma((2, 2, NY - 1)),
            dma((2,)), dma((2, NY)),
            dma((SETS,)), dma((SETS,)),
            dma((SETS,)), dma((SETS,)),
            dma((SETS,)), dma((SETS,)),
        ],
        compiler_params=pltpu.CompilerParams(
            collective_id=0, has_side_effects=True, vmem_limit_bytes=VMEM_MIB * 1024 * 1024
        ),
    )(queries, keys, values, block_mask, plan)


def solution(mesh):
    placed = (P(("blk", "uly"), None), P(("blk", "uly"), None), P(("blk", "uly"), None), P(), P())
    return jax.shard_map(
        body, mesh=mesh, in_specs=placed, out_specs=P(("blk", "uly"), None), check_vma=False
    )
```

```python
import functools
import math

import jax
import jax.numpy as jnp
from jax import lax
from jax.experimental import pallas as pl
from jax.experimental.pallas import tpu as pltpu
from jax.sharding import PartitionSpec as P

MESH = pl.DeviceIdType.MESH
H, HD, BT, TD = 24, 128, 128, 32
NX, NY, NZ = 4, 4, 8
NB = 64
HL = H // NZ
SETS = 3
RUN = NZ * TD
LANES = NX * RUN
BIG, FLOOR = 1e30, -1e29
VMEM_MIB = 62
NT = (((1,), (1,)), ((), ()))
RATE = math.log2(math.e) / math.sqrt(HD)
BF, F32 = jnp.bfloat16, jnp.float32
K, V, Q = 0, 1, 2


def kernel(
    q_in, k_in, v_in, mask_in, got,
    kb, vb, v_st, q_buf, m_st, shade, acc, top, tot, ob, ob_in, fin,
    us, ur, ul, ml, ys, yr, cs, cr, qs, qr, os_, or_, fs, fr, fl,
):
    u = lax.axis_index("uly")
    b = lax.axis_index("blk")
    core = u % 2
    z = b % NZ
    y = (b // NZ) % NY
    x = (u // 2) * 2 + b // (NZ * NY)

    def at(xx, yy, zz, cc):
        xx, yy, zz = xx % NX, yy % NY, zz % NZ
        return {"uly": (xx // 2) * 2 + cc, "blk": ((xx % 2) * NY + yy) * NZ + zz}

    same = [at(x, y, z + k, core) for k in range(NZ)]
    cross = [at(x, y, z + k, 1 - core) for k in range(NZ)]
    y_side = [at(x, y + d, z, core) for d in range(NY)]
    x_side = [at(x + d, y, z, core) for d in range(NX)]

    barrier = pltpu.get_barrier_semaphore()
    partners = same[1:] + cross + y_side[1:] + x_side[1:]
    for device in partners:
        pl.semaphore_signal(barrier, inc=1, device_id=device, device_id_type=MESH)

    mask_copy = pltpu.make_async_copy(mask_in.at[pl.ds(z * HL, HL)], m_st, ml)
    mask_copy.start()
    here = pl.ds(pl.multiple_of(z * TD, TD), TD)
    sources = (k_in, v_in, q_in)

    def place(a, i):
        if a == V:
            return v_st.at[i, here, :]
        if a == Q:
            return q_buf.at[i, here, :]
        return kb.at[i // 2, 0, i % 2, here, :]

    def columns_of(i, k):
        there = (z + k) % NZ
        lead = (2 * core, 2 - 2 * core, 1)[i]
        return pl.ds(pl.multiple_of((there * HL + lead) * HD, HD), HD)

    def own_in(a, i):
        return pltpu.make_async_copy(sources[a].at[:, columns_of(i, 0)], place(a, i), ul.at[a, i])

    for a in range(3):
        for i in (2, 0):
            own_in(a, i).start()
    pl.semaphore_wait(barrier, len(partners))

    def remote(src, dst, send, recv, device):
        return pltpu.make_async_remote_copy(
            src_ref=src, dst_ref=dst, send_sem=send, recv_sem=recv, device_id=device, device_id_type=MESH
        )

    def sum_of(ref, send, recv):
        return remote(ref, ref, send, recv, same[1])

    def first_of(i):
        return 0 if i == 1 else 1

    def entry(a, i, k):
        device = cross[k] if i == 1 else same[k]
        return remote(sources[a].at[:, columns_of(i, k)], place(a, i), us.at[a, i], ur.at[a, i], device)

    def entry_all(a, i):
        return sum_of(v_st.at[i, 0:(NZ - first_of(i)) * TD, :], us.at[a, i], ur.at[a, i])

    def send_in(a, i):
        for k in range(first_of(i), NZ):
            entry(a, i, k).start()

    def arrive(a, i):
        if i != 1:
            own_in(a, i).wait()
        entry_all(a, i).wait_recv()

    def y_copy(hk, a, half, d):
        buf = vb if a == V else kb
        return remote(
            buf.at[hk, 0, half], buf.at[hk, d, half], ys.at[hk, a], yr.at[hk, a, half, d - 1], y_side[NY - d]
        )

    def y_all(hk, a):
        ref = kb.at[0, 1:NY] if hk == 0 else kb.at[1, 1:NY, 0]
        return sum_of(ref, ys.at[hk, a], yr.at[hk, a, 0, 0])

    def c_copy(a, d):
        buf = vb if a == V else kb
        return remote(buf.at[1, d, 0], buf.at[1, d, 1], cs.at[a], cr.at[a, d], cross[0])

    def c_all(a):
        return sum_of(kb.at[1, 0:NY, 0], cs.at[a], cr.at[a, 0])

    def q_copy(i, d):
        return remote(
            q_buf.at[i, 0:RUN, :], q_buf.at[i, d * RUN:(d + 1) * RUN, :], qs.at[i], qr.at[i], x_side[NX - d]
        )

    def q_all(i):
        return sum_of(q_buf.at[i, RUN:LANES, :], qs.at[i], qr.at[i])

    def o_copy(i, d):
        return remote(ob.at[i, d - 1], ob_in.at[i, d - 1], os_.at[i], or_.at[i], x_side[d])

    def o_all(i):
        return sum_of(ob_in.at[i], os_.at[i], or_.at[i])

    mine = (z * HL + 2 * core, z * HL + 2 * core, z * HL + 1)

    def fin_copy(i, k):
        rows = pl.ds(pl.multiple_of(((z + k) % NZ) * TD, TD), TD)
        device = cross[k] if i == 1 else same[k]
        return remote(fin.at[i, rows, :], got.at[mine[i]], fs.at[i], fr.at[i], device)

    def own_out(i):
        return pltpu.make_async_copy(fin.at[i, here, :], got.at[mine[i]], fl.at[i])

    def fin_all(i):
        return sum_of(got.at[0:NZ - first_of(i)], fs.at[i], fr.at[i])

    def turn(i):
        for n in range(RUN // HD):
            rows = slice(n * HD, (n + 1) * HD)
            vb[i // 2, 0, i % 2, rows, :] = v_st[i, rows, :].T

    def scores(d, half, i, lo):
        return lax.dot_general(kb[i // 2, d, half], q_buf[i, lo:lo + BT, :], NT, preferred_element_type=F32)

    def soften(d, half, i, lo, score, first):
        lanes = slice(lo, lo + BT)
        bias = shade[i // 2, d, :, lanes]
        parts = [score[n * TD:(n + 1) * TD] for n in range(NZ)]
        tops = [jnp.max(p.reshape(TD // 8, 8, BT), axis=0) + bias[n:n + 1] for n, p in enumerate(parts)]
        new_top = jnp.maximum(jnp.max(functools.reduce(jnp.maximum, tops), axis=0, keepdims=True), FLOOR)
        fade = None
        if not first:
            old_top = top[i, :, lanes]
            new_top = jnp.maximum(new_top, old_top)
            fade = jnp.exp2((old_top - new_top) * RATE)
        shift = (bias - new_top) * RATE
        expo = [jnp.exp2(p * RATE + shift[n:n + 1]) for n, p in enumerate(parts)]
        top[i, :, lanes] = new_top
        return jnp.concatenate(expo, axis=0), fade

    def gather(d, half, i, lo, expo, fade):
        lanes = slice(lo, lo + BT)
        vals = jnp.concatenate([vb[i // 2, d, half, n * HD:(n + 1) * HD, :] for n in range(RUN // HD)], axis=1)
        update = jnp.dot(vals, expo.astype(BF), preferred_element_type=F32)
        total = jnp.sum(expo, axis=0, keepdims=True)
        if fade is not None:
            update = update + acc[i, :, lanes] * fade
            total = total + tot[i, :, lanes] * fade
        acc[i, :, lanes] = update
        tot[i, :, lanes] = total

    def unit(parts, first=False):
        todo = [(d, half, i, lo) for d, half, i in parts for lo in range(0, LANES, BT)]
        fresh = len(parts) if first is True else first
        score = scores(*todo[0])
        held = None
        for n, item in enumerate(todo):
            later = scores(*todo[n + 1]) if n + 1 < len(todo) else None
            soft = soften(*item, score, n < fresh * (LANES // BT))
            if held is not None:
                gather(*todo[n - 1], *held)
            held, score = soft, later
        gather(*todo[-1], *held)

    def split3(value):
        terms = []
        for _ in range(3):
            term = value.astype(BF).astype(F32)
            terms.append(term)
            value = value - term
        return terms

    def give_back(i):
        row = lax.broadcasted_iota(jnp.int32, (16, RUN), 0)
        for d in range(1, NX):
            lanes = slice(d * RUN, (d + 1) * RUN)
            ob[i, d - 1, 0:HD, :] = acc[i, :, lanes].astype(BF)
            notes = jnp.zeros((16, RUN), F32)
            for n, term in enumerate(split3(top[i, :, lanes]) + split3(tot[i, :, lanes])):
                notes = jnp.where(row == n, term, notes)
            ob[i, d - 1, HD:HD + 16, :] = notes.astype(BF)
            o_copy(i, d).start()

    def combine(i):
        o_all(i).wait_recv()
        own = slice(0, RUN)
        notes = [ob_in[i, d, HD:HD + 16, :].astype(F32) for d in range(NX - 1)]
        tops = [top[i, :, own]] + [n[0:1] + n[1:2] + n[2:3] for n in notes]
        tots = [tot[i, :, own]] + [n[3:4] + n[4:5] + n[5:6] for n in notes]
        best = functools.reduce(jnp.maximum, tops)
        fades = [jnp.exp2((t - best) * RATE) for t in tops]
        share = 1.0 / sum(f * t for f, t in zip(fades, tots))
        mixed = acc[i, :, own] * (fades[0] * share)
        for d in range(NX - 1):
            mixed = mixed + ob_in[i, d, 0:HD, :].astype(F32) * (fades[d + 1] * share)
        fin[i] = mixed.astype(BF).T
        for k in range(first_of(i), NZ):
            fin_copy(i, k).start()
        if i != 1:
            own_out(i).start()

    for a in (K, Q, V):
        send_in(a, 0)
        send_in(a, 1)
    for a in (K, V, Q):
        send_in(a, 2)

    for i in (0, 1):
        arrive(K, i)
    for d in (2, 1, 3):
        y_copy(0, K, 0, d).start()
        y_copy(0, K, 1, d).start()
    for i in (0, 1):
        arrive(Q, i)
        for d in (2, 1, 3):
            q_copy(i, d).start()
    for i in (0, 1):
        arrive(V, i)
        turn(i)
        for d in (2, 1, 3):
            y_copy(0, V, i, d).start()
    arrive(K, 2)
    for d in (2, 1, 3):
        y_copy(1, K, 0, d).start()
    c_copy(K, 0).start()
    arrive(V, 2)
    turn(2)
    for d in (2, 1, 3):
        y_copy(1, V, 0, d).start()
    c_copy(V, 0).start()
    arrive(Q, 2)
    for d in (2, 1, 3):
        q_copy(2, d).start()

    mask_copy.wait()
    key_row = lax.broadcasted_iota(jnp.int32, (NY * NZ, NB), 0)
    key_col = lax.broadcasted_iota(jnp.int32, (NY * NZ, NB), 1)
    key_block = ((x % 2) * NY + (y + key_row // NZ) % NY) * NZ + key_row % NZ
    pick_key = (key_col == key_block).astype(F32).astype(BF)
    run_row = lax.broadcasted_iota(jnp.int32, (NB, LANES), 0)
    run_col = lax.broadcasted_iota(jnp.int32, (NB, LANES), 1)
    run_block = (((x + run_col // RUN) % 2) * NY + y) * NZ + (run_col // TD) % NZ
    pick_run = (run_row == run_block).astype(F32).astype(BF)
    for hk in range(2):
        allowed = (m_st[2 * core if hk == 0 else 1] > 0).astype(F32).astype(BF)
        rows = lax.dot_general(pick_key, allowed, NT, preferred_element_type=F32).astype(BF)
        rows = jnp.dot(rows, pick_run, preferred_element_type=F32)
        rows = jnp.where(rows > 0.5, 0.0, -BIG)
        for d in range(NY):
            shade[hk, d] = rows[d * NZ:(d + 1) * NZ, :]

    for i in (0, 1):
        q_all(i).wait_recv()
    unit([(0, half, i) for half in (0, 1) for i in (0, 1)], first=2)
    for half in (0, 1):
        for d in (2, 1, 3):
            y_copy(0, K, half, d).wait_recv()
            y_copy(0, V, half, d).wait_recv()
            unit([(d, half, i) for i in (0, 1)])
    for i in (0, 1):
        give_back(i)
    for d in (2, 1, 3):
        y_copy(1, K, 0, d).wait_recv()
        c_copy(K, d).start()
    q_all(2).wait_recv()
    for a in (K, V):
        c_copy(a, 0).wait_recv()
    unit([(0, 0, 2), (0, 1, 2)], first=1)
    for d in (2, 1, 3):
        y_copy(1, V, 0, d).wait_recv()
        c_copy(V, d).start()
    unit([(d, 0, 2) for d in (2, 1, 3)])
    for d in (2, 1, 3):
        for a in (K, V):
            c_copy(a, d).wait_recv()
    unit([(d, 1, 2) for d in (2, 1, 3)])
    give_back(2)
    combine(0)
    combine(1)
    for i in range(SETS):
        for a in range(3):
            entry_all(a, i).wait_send()
        q_all(i).wait_send()
    for a in (K, V):
        y_all(0, a).wait_send()
        y_all(1, a).wait_send()
        c_all(a).wait_send()
    combine(2)
    for i in range(SETS):
        o_all(i).wait_send()
    for i in range(SETS):
        fin_all(i).wait_recv()
    for i in range(SETS):
        fin_all(i).wait_send()
        if i != 1:
            own_out(i).wait()


def body(queries, keys, values, block_mask, plan):
    dma = pltpu.SemaphoreType.DMA
    hbm = pl.BlockSpec(memory_space=pl.ANY)
    heads = pl.pallas_call(
        kernel,
        out_shape=jax.ShapeDtypeStruct((H, TD, HD), BF),
        in_specs=[hbm, hbm, hbm, hbm],
        out_specs=hbm,
        scratch_shapes=[
            pltpu.VMEM((2, NY, 2, RUN, HD), BF),
            pltpu.VMEM((2, NY, 2, RUN, HD), BF),
            pltpu.VMEM((SETS, RUN, HD), BF),
            pltpu.VMEM((SETS, LANES, HD), BF),
            pltpu.VMEM((HL, NB, NB), jnp.int32),
            pltpu.VMEM((2, NY, NZ, LANES), F32),
            pltpu.VMEM((SETS, HD, LANES), F32),
            pltpu.VMEM((SETS, 1, LANES), F32),
            pltpu.VMEM((SETS, 1, LANES), F32),
            pltpu.VMEM((SETS, NX - 1, HD + 16, RUN), BF),
            pltpu.VMEM((SETS, NX - 1, HD + 16, RUN), BF),
            pltpu.VMEM((SETS, RUN, HD), BF),
            dma((3, SETS)), dma((3, SETS)), dma((3, SETS)), dma,
            dma((2, 2)), dma((2, 2, 2, NY - 1)),
            dma((2,)), dma((2, NY)),
            dma((SETS,)), dma((SETS,)),
            dma((SETS,)), dma((SETS,)),
            dma((SETS,)), dma((SETS,)), dma((SETS,)),
        ],
        compiler_params=pltpu.CompilerParams(
            collective_id=0, has_side_effects=True, vmem_limit_bytes=VMEM_MIB * 1024 * 1024
        ),
    )(queries, keys, values, block_mask)
    return jnp.transpose(heads.at[plan].get(mode="promise_in_bounds"), (1, 0, 2)).reshape(queries.shape)


def solution(mesh):
    placed = (P(("blk", "uly"), None), P(("blk", "uly"), None), P(("blk", "uly"), None), P(), P())
    return jax.shard_map(
        body, mesh=mesh, in_specs=placed, out_specs=P(("blk", "uly"), None), check_vma=False
    )
```

```python
import functools
import math

import jax
import jax.numpy as jnp
from jax import lax
from jax.experimental import pallas as pl
from jax.experimental.pallas import tpu as pltpu
from jax.sharding import PartitionSpec as P

MESH = pl.DeviceIdType.MESH
H, HD, BT, TD = 24, 128, 128, 32
NX, NY, NZ = 4, 4, 8
NB = 64
HL = H // NZ
SETS = 3
RUN = NZ * TD
LANES = NX * RUN
BIG, FLOOR = 1e30, -1e29
VMEM_MIB = 62
NT = (((1,), (1,)), ((), ()))
RATE = math.log2(math.e) / math.sqrt(HD)
BF, F32 = jnp.bfloat16, jnp.float32
K, V, Q = 0, 1, 2


def kernel(
    q_in, k_in, v_in, mask_in, got,
    kb, vb, v_st, q_buf, m_st, shade, acc, top, tot, ob, ob_in, fin,
    us, ur, ul, ml, ys, yr, cs, cr, qs, qr, os_, or_, fs, fr, fl,
):
    u = lax.axis_index("uly")
    b = lax.axis_index("blk")
    core = u % 2
    z = b % NZ
    y = (b // NZ) % NY
    x = (u // 2) * 2 + b // (NZ * NY)

    def at(xx, yy, zz, cc):
        xx, yy, zz = xx % NX, yy % NY, zz % NZ
        return {"uly": (xx // 2) * 2 + cc, "blk": ((xx % 2) * NY + yy) * NZ + zz}

    same = [at(x, y, z + k, core) for k in range(NZ)]
    cross = [at(x, y, z + k, 1 - core) for k in range(NZ)]
    y_side = [at(x, y + d, z, core) for d in range(NY)]
    x_side = [at(x + d, y, z, core) for d in range(NX)]

    barrier = pltpu.get_barrier_semaphore()
    partners = same[1:] + cross + y_side[1:] + x_side[1:]
    for device in partners:
        pl.semaphore_signal(barrier, inc=1, device_id=device, device_id_type=MESH)

    mask_copy = pltpu.make_async_copy(mask_in.at[pl.ds(z * HL, HL)], m_st, ml)
    mask_copy.start()
    here = pl.ds(pl.multiple_of(z * TD, TD), TD)
    sources = (k_in, v_in, q_in)

    def place(a, i):
        if a == V:
            return v_st.at[i, here, :]
        if a == Q:
            return q_buf.at[i, here, :]
        return kb.at[i // 2, 0, i % 2, here, :]

    def columns_of(i, k):
        there = (z + k) % NZ
        lead = (2 * core, 2 - 2 * core, 1)[i]
        return pl.ds(pl.multiple_of((there * HL + lead) * HD, HD), HD)

    def own_in(a, i):
        return pltpu.make_async_copy(sources[a].at[:, columns_of(i, 0)], place(a, i), ul.at[a, i])

    for a in range(3):
        for i in (2, 0):
            own_in(a, i).start()
    pl.semaphore_wait(barrier, len(partners))

    def remote(src, dst, send, recv, device):
        return pltpu.make_async_remote_copy(
            src_ref=src, dst_ref=dst, send_sem=send, recv_sem=recv, device_id=device, device_id_type=MESH
        )

    def sum_of(ref, send, recv):
        return remote(ref, ref, send, recv, same[1])

    def first_of(i):
        return 0 if i == 1 else 1

    def entry(a, i, k):
        device = cross[k] if i == 1 else same[k]
        return remote(sources[a].at[:, columns_of(i, k)], place(a, i), us.at[a, i], ur.at[a, i], device)

    def entry_all(a, i):
        return sum_of(v_st.at[i, 0:(NZ - first_of(i)) * TD, :], us.at[a, i], ur.at[a, i])

    def send_in(a, i):
        for k in range(first_of(i), NZ):
            entry(a, i, k).start()

    def arrive(a, i):
        if i != 1:
            own_in(a, i).wait()
        entry_all(a, i).wait_recv()

    def y_copy(hk, a, half, d):
        buf = vb if a == V else kb
        return remote(
            buf.at[hk, 0, half], buf.at[hk, d, half], ys.at[hk, a], yr.at[hk, a, half, d - 1], y_side[NY - d]
        )

    def y_all(hk, a):
        ref = kb.at[0, 1:NY] if hk == 0 else kb.at[1, 1:NY, 0]
        return sum_of(ref, ys.at[hk, a], yr.at[hk, a, 0, 0])

    def c_copy(a, d):
        buf = vb if a == V else kb
        return remote(buf.at[1, d, 0], buf.at[1, d, 1], cs.at[a], cr.at[a, d], cross[0])

    def c_all(a):
        return sum_of(kb.at[1, 0:NY, 0], cs.at[a], cr.at[a, 0])

    def q_copy(i, d):
        return remote(
            q_buf.at[i, 0:RUN, :], q_buf.at[i, d * RUN:(d + 1) * RUN, :], qs.at[i], qr.at[i], x_side[NX - d]
        )

    def q_all(i):
        return sum_of(q_buf.at[i, RUN:LANES, :], qs.at[i], qr.at[i])

    def o_copy(i, d):
        return remote(ob.at[i, d - 1], ob_in.at[i, d - 1], os_.at[i], or_.at[i], x_side[d])

    def o_all(i):
        return sum_of(ob_in.at[i], os_.at[i], or_.at[i])

    mine = (z * HL + 2 * core, z * HL + 2 * core, z * HL + 1)

    def fin_copy(i, k):
        rows = pl.ds(pl.multiple_of(((z + k) % NZ) * TD, TD), TD)
        device = cross[k] if i == 1 else same[k]
        return remote(fin.at[i, rows, :], got.at[mine[i]], fs.at[i], fr.at[i], device)

    def own_out(i):
        return pltpu.make_async_copy(fin.at[i, here, :], got.at[mine[i]], fl.at[i])

    def fin_all(i):
        return sum_of(got.at[0:NZ - first_of(i)], fs.at[i], fr.at[i])

    def turn(i):
        for n in range(RUN // HD):
            rows = slice(n * HD, (n + 1) * HD)
            vb[i // 2, 0, i % 2, rows, :] = v_st[i, rows, :].T

    def scores(d, half, i, lo):
        return lax.dot_general(kb[i // 2, d, half], q_buf[i, lo:lo + BT, :], NT, preferred_element_type=F32)

    def soften(d, half, i, lo, score, first):
        lanes = slice(lo, lo + BT)
        bias = shade[i // 2, d, :, lanes]
        parts = [score[n * TD:(n + 1) * TD] for n in range(NZ)]
        tops = [jnp.max(p.reshape(TD // 8, 8, BT), axis=0) + bias[n:n + 1] for n, p in enumerate(parts)]
        new_top = jnp.maximum(jnp.max(functools.reduce(jnp.maximum, tops), axis=0, keepdims=True), FLOOR)
        fade = None
        if not first:
            old_top = top[i, :, lanes]
            new_top = jnp.maximum(new_top, old_top)
            fade = jnp.exp2((old_top - new_top) * RATE)
        shift = (bias - new_top) * RATE
        expo = [jnp.exp2(p * RATE + shift[n:n + 1]) for n, p in enumerate(parts)]
        top[i, :, lanes] = new_top
        return jnp.concatenate(expo, axis=0), fade

    def gather(d, half, i, lo, expo, fade):
        lanes = slice(lo, lo + BT)
        vals = jnp.concatenate([vb[i // 2, d, half, n * HD:(n + 1) * HD, :] for n in range(RUN // HD)], axis=1)
        update = jnp.dot(vals, expo.astype(BF), preferred_element_type=F32)
        total = jnp.sum(expo, axis=0, keepdims=True)
        if fade is not None:
            update = update + acc[i, :, lanes] * fade
            total = total + tot[i, :, lanes] * fade
        acc[i, :, lanes] = update
        tot[i, :, lanes] = total

    def unit(parts, first=False):
        todo = [(d, half, i, lo) for d, half, i in parts for lo in range(0, LANES, BT)]
        fresh = len(parts) if first is True else first
        score = scores(*todo[0])
        held = None
        for n, item in enumerate(todo):
            later = scores(*todo[n + 1]) if n + 1 < len(todo) else None
            soft = soften(*item, score, n < fresh * (LANES // BT))
            if held is not None:
                gather(*todo[n - 1], *held)
            held, score = soft, later
        gather(*todo[-1], *held)

    def split3(value):
        terms = []
        for _ in range(3):
            term = value.astype(BF).astype(F32)
            terms.append(term)
            value = value - term
        return terms

    def give_back(i):
        row = lax.broadcasted_iota(jnp.int32, (16, RUN), 0)
        for d in (2, 1, 3):
            lanes = slice(d * RUN, (d + 1) * RUN)
            ob[i, d - 1, 0:HD, :] = acc[i, :, lanes].astype(BF)
            notes = jnp.zeros((16, RUN), F32)
            for n, term in enumerate(split3(top[i, :, lanes]) + split3(tot[i, :, lanes])):
                notes = jnp.where(row == n, term, notes)
            ob[i, d - 1, HD:HD + 16, :] = notes.astype(BF)
            o_copy(i, d).start()

    def combine(i):
        o_all(i).wait_recv()
        own = slice(0, RUN)
        notes = [ob_in[i, d, HD:HD + 16, :].astype(F32) for d in range(NX - 1)]
        tops = [top[i, :, own]] + [n[0:1] + n[1:2] + n[2:3] for n in notes]
        tots = [tot[i, :, own]] + [n[3:4] + n[4:5] + n[5:6] for n in notes]
        best = functools.reduce(jnp.maximum, tops)
        fades = [jnp.exp2((t - best) * RATE) for t in tops]
        share = 1.0 / sum(f * t for f, t in zip(fades, tots))
        mixed = acc[i, :, own] * (fades[0] * share)
        for d in range(NX - 1):
            mixed = mixed + ob_in[i, d, 0:HD, :].astype(F32) * (fades[d + 1] * share)
        fin[i] = mixed.astype(BF).T
        for k in range(first_of(i), NZ):
            fin_copy(i, k).start()
        if i != 1:
            own_out(i).start()

    for a in (K, Q, V):
        send_in(a, 0)
        send_in(a, 1)
    for a in (K, V, Q):
        send_in(a, 2)

    for i in (0, 1):
        arrive(K, i)
        for d in (2, 1, 3):
            y_copy(0, K, i, d).start()
    for i in (0, 1):
        arrive(Q, i)
        for d in (2, 1, 3):
            q_copy(i, d).start()
    for i in (0, 1):
        arrive(V, i)
        turn(i)
        for d in (2, 1, 3):
            y_copy(0, V, i, d).start()
    arrive(K, 2)
    for d in (2, 1, 3):
        y_copy(1, K, 0, d).start()
    c_copy(K, 0).start()
    arrive(V, 2)
    turn(2)
    for d in (2, 1, 3):
        y_copy(1, V, 0, d).start()
    c_copy(V, 0).start()
    arrive(Q, 2)
    for d in (2, 1, 3):
        q_copy(2, d).start()

    mask_copy.wait()
    key_row = lax.broadcasted_iota(jnp.int32, (NY * NZ, NB), 0)
    key_col = lax.broadcasted_iota(jnp.int32, (NY * NZ, NB), 1)
    key_block = ((x % 2) * NY + (y + key_row // NZ) % NY) * NZ + key_row % NZ
    pick_key = (key_col == key_block).astype(F32).astype(BF)
    run_row = lax.broadcasted_iota(jnp.int32, (NB, LANES), 0)
    run_col = lax.broadcasted_iota(jnp.int32, (NB, LANES), 1)
    run_block = (((x + run_col // RUN) % 2) * NY + y) * NZ + (run_col // TD) % NZ
    pick_run = (run_row == run_block).astype(F32).astype(BF)
    for hk in range(2):
        allowed = (m_st[2 * core if hk == 0 else 1] > 0).astype(F32).astype(BF)
        rows = lax.dot_general(pick_key, allowed, NT, preferred_element_type=F32).astype(BF)
        rows = jnp.dot(rows, pick_run, preferred_element_type=F32)
        rows = jnp.where(rows > 0.5, 0.0, -BIG)
        for d in range(NY):
            shade[hk, d] = rows[d * NZ:(d + 1) * NZ, :]

    for i in (0, 1):
        q_all(i).wait_recv()
    unit([(0, half, i) for half in (0, 1) for i in (0, 1)], first=2)
    for half in (0, 1):
        for d in (2, 1, 3):
            y_copy(0, K, half, d).wait_recv()
            y_copy(0, V, half, d).wait_recv()
            unit([(d, half, i) for i in (0, 1)])
    for i in (0, 1):
        give_back(i)
    for d in (2, 1, 3):
        y_copy(1, K, 0, d).wait_recv()
        c_copy(K, d).start()
    q_all(2).wait_recv()
    for a in (K, V):
        c_copy(a, 0).wait_recv()
    unit([(0, 0, 2), (0, 1, 2)], first=1)
    for d in (2, 1, 3):
        y_copy(1, V, 0, d).wait_recv()
        c_copy(V, d).start()
    unit([(d, 0, 2) for d in (2, 1, 3)])
    for d in (2, 1, 3):
        for a in (K, V):
            c_copy(a, d).wait_recv()
    unit([(d, 1, 2) for d in (2, 1, 3)])
    give_back(2)
    combine(0)
    combine(1)
    for i in range(SETS):
        for a in range(3):
            entry_all(a, i).wait_send()
        q_all(i).wait_send()
    for a in (K, V):
        y_all(0, a).wait_send()
        y_all(1, a).wait_send()
        c_all(a).wait_send()
    combine(2)
    for i in range(SETS):
        o_all(i).wait_send()
    for i in range(SETS):
        fin_all(i).wait_recv()
    for i in range(SETS):
        fin_all(i).wait_send()
        if i != 1:
            own_out(i).wait()


def arrange(plan_s, heads, out):
    for s in range(H):
        out[:, s * HD:(s + 1) * HD] = heads[plan_s[s]]


def body(queries, keys, values, block_mask, plan):
    dma = pltpu.SemaphoreType.DMA
    hbm = pl.BlockSpec(memory_space=pl.ANY)
    heads = pl.pallas_call(
        kernel,
        out_shape=jax.ShapeDtypeStruct((H, TD, HD), BF),
        in_specs=[hbm, hbm, hbm, hbm],
        out_specs=hbm,
        scratch_shapes=[
            pltpu.VMEM((2, NY, 2, RUN, HD), BF),
            pltpu.VMEM((2, NY, 2, RUN, HD), BF),
            pltpu.VMEM((SETS, RUN, HD), BF),
            pltpu.VMEM((SETS, LANES, HD), BF),
            pltpu.VMEM((HL, NB, NB), jnp.int32),
            pltpu.VMEM((2, NY, NZ, LANES), F32),
            pltpu.VMEM((SETS, HD, LANES), F32),
            pltpu.VMEM((SETS, 1, LANES), F32),
            pltpu.VMEM((SETS, 1, LANES), F32),
            pltpu.VMEM((SETS, NX - 1, HD + 16, RUN), BF),
            pltpu.VMEM((SETS, NX - 1, HD + 16, RUN), BF),
            pltpu.VMEM((SETS, RUN, HD), BF),
            dma((3, SETS)), dma((3, SETS)), dma((3, SETS)), dma,
            dma((2, 2)), dma((2, 2, 2, NY - 1)),
            dma((2,)), dma((2, NY)),
            dma((SETS,)), dma((SETS,)),
            dma((SETS,)), dma((SETS,)),
            dma((SETS,)), dma((SETS,)), dma((SETS,)),
        ],
        compiler_params=pltpu.CompilerParams(
            collective_id=0, has_side_effects=True, vmem_limit_bytes=VMEM_MIB * 1024 * 1024
        ),
    )(queries, keys, values, block_mask)
    whole = pl.BlockSpec(memory_space=pltpu.VMEM)
    return pl.pallas_call(
        arrange,
        out_shape=jax.ShapeDtypeStruct(queries.shape, BF),
        in_specs=[pl.BlockSpec(memory_space=pltpu.SMEM), whole],
        out_specs=whole,
    )(plan, heads)


def solution(mesh):
    placed = (P(("blk", "uly"), None), P(("blk", "uly"), None), P(("blk", "uly"), None), P(), P())
    return jax.shard_map(
        body, mesh=mesh, in_specs=placed, out_specs=P(("blk", "uly"), None), check_vma=False
    )
```

```python
import functools
import math

import jax
import jax.numpy as jnp
from jax import lax
from jax.experimental import pallas as pl
from jax.experimental.pallas import tpu as pltpu
from jax.sharding import PartitionSpec as P

MESH = pl.DeviceIdType.MESH
H, HD, BT, TD = 24, 128, 128, 32
NX, NY, NZ = 4, 4, 8
NB = 64
HL = H // NZ
SETS = 3
RUN = NZ * TD
LANES = NX * RUN
BIG, FLOOR = 1e30, -1e29
VMEM_MIB = 62
NT = (((1,), (1,)), ((), ()))
RATE = math.log2(math.e) / math.sqrt(HD)
BF, F32 = jnp.bfloat16, jnp.float32
K, V, Q = 0, 1, 2


def kernel(
    q_in, k_in, v_in, mask_in, got,
    kb, vb, v_st, q_buf, m_st, shade, acc, top, tot, ob, ob_in, fin,
    us, ur, ul, ml, ys, yr, cs, cr, qs, qr, os_, or_, fs, fr, fl,
):
    u = lax.axis_index("uly")
    b = lax.axis_index("blk")
    core = u % 2
    z = b % NZ
    y = (b // NZ) % NY
    x = (u // 2) * 2 + b // (NZ * NY)

    def at(xx, yy, zz, cc):
        xx, yy, zz = xx % NX, yy % NY, zz % NZ
        return {"uly": (xx // 2) * 2 + cc, "blk": ((xx % 2) * NY + yy) * NZ + zz}

    same = [at(x, y, z + k, core) for k in range(NZ)]
    cross = [at(x, y, z + k, 1 - core) for k in range(NZ)]
    y_side = [at(x, y + d, z, core) for d in range(NY)]
    x_side = [at(x + d, y, z, core) for d in range(NX)]

    barrier = pltpu.get_barrier_semaphore()
    partners = same[1:] + cross + y_side[1:] + x_side[1:]
    for device in partners:
        pl.semaphore_signal(barrier, inc=1, device_id=device, device_id_type=MESH)

    mask_copy = pltpu.make_async_copy(mask_in.at[pl.ds(z * HL, HL)], m_st, ml)
    mask_copy.start()
    here = pl.ds(pl.multiple_of(z * TD, TD), TD)
    sources = (k_in, v_in, q_in)

    def place(a, i):
        if a == V:
            return v_st.at[i, here, :]
        if a == Q:
            return q_buf.at[i, here, :]
        return kb.at[i // 2, 0, i % 2, here, :]

    def columns_of(i, k):
        there = (z + k) % NZ
        lead = (2 * core, 2 - 2 * core, 1)[i]
        return pl.ds(pl.multiple_of((there * HL + lead) * HD, HD), HD)

    def own_in(a, i):
        return pltpu.make_async_copy(sources[a].at[:, columns_of(i, 0)], place(a, i), ul.at[a, i])

    for a in range(3):
        for i in (2, 0):
            own_in(a, i).start()
    pl.semaphore_wait(barrier, len(partners))

    def remote(src, dst, send, recv, device):
        return pltpu.make_async_remote_copy(
            src_ref=src, dst_ref=dst, send_sem=send, recv_sem=recv, device_id=device, device_id_type=MESH
        )

    def sum_of(ref, send, recv):
        return remote(ref, ref, send, recv, same[1])

    far = (4, 3, 5, 2, 6, 1, 7)

    def first_of(i):
        return 0 if i == 1 else 1

    def entry(a, i, k):
        device = cross[k] if i == 1 else same[k]
        return remote(sources[a].at[:, columns_of(i, k)], place(a, i), us.at[a, i], ur.at[a, i], device)

    def entry_all(a, i):
        return sum_of(v_st.at[i, 0:(NZ - first_of(i)) * TD, :], us.at[a, i], ur.at[a, i])

    def send_in(a, i):
        for k in far if i != 1 else far + (0,):
            entry(a, i, k).start()

    def arrive(a, i):
        if i != 1:
            own_in(a, i).wait()
        entry_all(a, i).wait_recv()

    def y_copy(hk, a, half, d):
        buf = vb if a == V else kb
        return remote(
            buf.at[hk, 0, half], buf.at[hk, d, half], ys.at[hk, a], yr.at[hk, a, half, d - 1], y_side[NY - d]
        )

    def y_all(hk, a):
        ref = kb.at[0, 1:NY] if hk == 0 else kb.at[1, 1:NY, 0]
        return sum_of(ref, ys.at[hk, a], yr.at[hk, a, 0, 0])

    def c_copy(a, d):
        buf = vb if a == V else kb
        return remote(buf.at[1, d, 0], buf.at[1, d, 1], cs.at[a], cr.at[a, d], cross[0])

    def c_all(a):
        return sum_of(kb.at[1, 0:NY, 0], cs.at[a], cr.at[a, 0])

    def q_copy(i, d):
        return remote(
            q_buf.at[i, 0:RUN, :], q_buf.at[i, d * RUN:(d + 1) * RUN, :], qs.at[i], qr.at[i], x_side[NX - d]
        )

    def q_all(i):
        return sum_of(q_buf.at[i, RUN:LANES, :], qs.at[i], qr.at[i])

    def o_copy(i, d):
        return remote(ob.at[i, d - 1], ob_in.at[i, d - 1], os_.at[i], or_.at[i], x_side[d])

    def o_all(i):
        return sum_of(ob_in.at[i], os_.at[i], or_.at[i])

    mine = (z * HL + 2 * core, z * HL + 2 * core, z * HL + 1)

    def fin_copy(i, k):
        rows = pl.ds(pl.multiple_of(((z + k) % NZ) * TD, TD), TD)
        device = cross[k] if i == 1 else same[k]
        return remote(fin.at[i, rows, :], got.at[mine[i]], fs.at[i], fr.at[i], device)

    def own_out(i):
        return pltpu.make_async_copy(fin.at[i, here, :], got.at[mine[i]], fl.at[i])

    def fin_all(i):
        return sum_of(got.at[0:NZ - first_of(i)], fs.at[i], fr.at[i])

    def turn(i):
        for n in range(RUN // HD):
            rows = slice(n * HD, (n + 1) * HD)
            vb[i // 2, 0, i % 2, rows, :] = v_st[i, rows, :].T

    def scores(d, half, i, lo):
        return lax.dot_general(kb[i // 2, d, half], q_buf[i, lo:lo + BT, :], NT, preferred_element_type=F32)

    def soften(d, half, i, lo, score, first):
        lanes = slice(lo, lo + BT)
        bias = shade[i // 2, d, :, lanes]
        parts = [score[n * TD:(n + 1) * TD] for n in range(NZ)]
        tops = [jnp.max(p.reshape(TD // 8, 8, BT), axis=0) + bias[n:n + 1] for n, p in enumerate(parts)]
        new_top = jnp.maximum(jnp.max(functools.reduce(jnp.maximum, tops), axis=0, keepdims=True), FLOOR)
        fade = None
        if not first:
            old_top = top[i, :, lanes]
            new_top = jnp.maximum(new_top, old_top)
            fade = jnp.exp2((old_top - new_top) * RATE)
        shift = (bias - new_top) * RATE
        expo = [jnp.exp2(p * RATE + shift[n:n + 1]) for n, p in enumerate(parts)]
        top[i, :, lanes] = new_top
        return jnp.concatenate(expo, axis=0), fade

    def gather(d, half, i, lo, expo, fade):
        lanes = slice(lo, lo + BT)
        vals = jnp.concatenate([vb[i // 2, d, half, n * HD:(n + 1) * HD, :] for n in range(RUN // HD)], axis=1)
        update = jnp.dot(vals, expo.astype(BF), preferred_element_type=F32)
        total = jnp.sum(expo, axis=0, keepdims=True)
        if fade is not None:
            update = update + acc[i, :, lanes] * fade
            total = total + tot[i, :, lanes] * fade
        acc[i, :, lanes] = update
        tot[i, :, lanes] = total

    def unit(parts, first=False):
        todo = [(d, half, i, lo) for d, half, i in parts for lo in range(0, LANES, BT)]
        fresh = len(parts) if first is True else first
        score = scores(*todo[0])
        held = None
        for n, item in enumerate(todo):
            later = scores(*todo[n + 1]) if n + 1 < len(todo) else None
            soft = soften(*item, score, n < fresh * (LANES // BT))
            if held is not None:
                gather(*todo[n - 1], *held)
            held, score = soft, later
        gather(*todo[-1], *held)

    def split3(value):
        terms = []
        for _ in range(3):
            term = value.astype(BF).astype(F32)
            terms.append(term)
            value = value - term
        return terms

    def give_back(i):
        row = lax.broadcasted_iota(jnp.int32, (16, RUN), 0)
        for d in (2, 1, 3):
            lanes = slice(d * RUN, (d + 1) * RUN)
            ob[i, d - 1, 0:HD, :] = acc[i, :, lanes].astype(BF)
            notes = jnp.zeros((16, RUN), F32)
            for n, term in enumerate(split3(top[i, :, lanes]) + split3(tot[i, :, lanes])):
                notes = jnp.where(row == n, term, notes)
            ob[i, d - 1, HD:HD + 16, :] = notes.astype(BF)
            o_copy(i, d).start()

    def combine(i):
        o_all(i).wait_recv()
        own = slice(0, RUN)
        notes = [ob_in[i, d, HD:HD + 16, :].astype(F32) for d in range(NX - 1)]
        tops = [top[i, :, own]] + [n[0:1] + n[1:2] + n[2:3] for n in notes]
        tots = [tot[i, :, own]] + [n[3:4] + n[4:5] + n[5:6] for n in notes]
        best = functools.reduce(jnp.maximum, tops)
        fades = [jnp.exp2((t - best) * RATE) for t in tops]
        share = 1.0 / sum(f * t for f, t in zip(fades, tots))
        mixed = acc[i, :, own] * (fades[0] * share)
        for d in range(NX - 1):
            mixed = mixed + ob_in[i, d, 0:HD, :].astype(F32) * (fades[d + 1] * share)
        fin[i] = mixed.astype(BF).T
        for k in far if i != 1 else far + (0,):
            fin_copy(i, k).start()
        if i != 1:
            own_out(i).start()

    for a in (K, Q, V):
        send_in(a, 0)
        send_in(a, 1)
    for a in (K, V, Q):
        send_in(a, 2)

    for i in (0, 1):
        arrive(K, i)
        for d in (2, 1, 3):
            y_copy(0, K, i, d).start()
    for i in (0, 1):
        arrive(Q, i)
        for d in (2, 1, 3):
            q_copy(i, d).start()
    for i in (0, 1):
        arrive(V, i)
        turn(i)
        for d in (2, 1, 3):
            y_copy(0, V, i, d).start()
    arrive(K, 2)
    for d in (2, 1, 3):
        y_copy(1, K, 0, d).start()
    c_copy(K, 0).start()
    arrive(V, 2)
    turn(2)
    for d in (2, 1, 3):
        y_copy(1, V, 0, d).start()
    c_copy(V, 0).start()
    arrive(Q, 2)
    for d in (2, 1, 3):
        q_copy(2, d).start()

    mask_copy.wait()
    key_row = lax.broadcasted_iota(jnp.int32, (NY * NZ, NB), 0)
    key_col = lax.broadcasted_iota(jnp.int32, (NY * NZ, NB), 1)
    key_block = ((x % 2) * NY + (y + key_row // NZ) % NY) * NZ + key_row % NZ
    pick_key = (key_col == key_block).astype(F32).astype(BF)
    run_row = lax.broadcasted_iota(jnp.int32, (NB, LANES), 0)
    run_col = lax.broadcasted_iota(jnp.int32, (NB, LANES), 1)
    run_block = (((x + run_col // RUN) % 2) * NY + y) * NZ + (run_col // TD) % NZ
    pick_run = (run_row == run_block).astype(F32).astype(BF)
    for hk in range(2):
        allowed = (m_st[2 * core if hk == 0 else 1] > 0).astype(F32).astype(BF)
        rows = lax.dot_general(pick_key, allowed, NT, preferred_element_type=F32).astype(BF)
        rows = jnp.dot(rows, pick_run, preferred_element_type=F32)
        rows = jnp.where(rows > 0.5, 0.0, -BIG)
        for d in range(NY):
            shade[hk, d] = rows[d * NZ:(d + 1) * NZ, :]

    for i in (0, 1):
        q_all(i).wait_recv()
    unit([(0, half, i) for half in (0, 1) for i in (0, 1)], first=2)
    for half, d in ((0, 2), (0, 1), (0, 3), (1, 2)):
        y_copy(0, K, half, d).wait_recv()
        y_copy(0, V, half, d).wait_recv()
        unit([(d, half, i) for i in (0, 1)])
    for d in (1, 3):
        y_copy(0, K, 1, d).wait_recv()
        y_copy(0, V, 1, d).wait_recv()
    for i in (0, 1):
        unit([(d, 1, i) for d in (1, 3)])
        give_back(i)
    for d in (2, 1, 3):
        y_copy(1, K, 0, d).wait_recv()
        c_copy(K, d).start()
    q_all(2).wait_recv()
    for a in (K, V):
        c_copy(a, 0).wait_recv()
    unit([(0, 0, 2), (0, 1, 2)], first=1)
    for d in (2, 1, 3):
        y_copy(1, V, 0, d).wait_recv()
        c_copy(V, d).start()
    unit([(d, 0, 2) for d in (2, 1, 3)])
    for d in (2, 1, 3):
        for a in (K, V):
            c_copy(a, d).wait_recv()
    unit([(d, 1, 2) for d in (2, 1, 3)])
    give_back(2)
    combine(0)
    combine(1)
    for i in range(SETS):
        for a in range(3):
            entry_all(a, i).wait_send()
        q_all(i).wait_send()
    for a in (K, V):
        y_all(0, a).wait_send()
        y_all(1, a).wait_send()
        c_all(a).wait_send()
    combine(2)
    for i in range(SETS):
        o_all(i).wait_send()
    for i in range(SETS):
        fin_all(i).wait_recv()
    for i in range(SETS):
        fin_all(i).wait_send()
        if i != 1:
            own_out(i).wait()


def arrange(plan_s, heads, out):
    for s in range(H):
        out[:, s * HD:(s + 1) * HD] = heads[plan_s[s]]


def body(queries, keys, values, block_mask, plan):
    dma = pltpu.SemaphoreType.DMA
    hbm = pl.BlockSpec(memory_space=pl.ANY)
    heads = pl.pallas_call(
        kernel,
        out_shape=jax.ShapeDtypeStruct((H, TD, HD), BF),
        in_specs=[hbm, hbm, hbm, hbm],
        out_specs=hbm,
        scratch_shapes=[
            pltpu.VMEM((2, NY, 2, RUN, HD), BF),
            pltpu.VMEM((2, NY, 2, RUN, HD), BF),
            pltpu.VMEM((SETS, RUN, HD), BF),
            pltpu.VMEM((SETS, LANES, HD), BF),
            pltpu.VMEM((HL, NB, NB), jnp.int32),
            pltpu.VMEM((2, NY, NZ, LANES), F32),
            pltpu.VMEM((SETS, HD, LANES), F32),
            pltpu.VMEM((SETS, 1, LANES), F32),
            pltpu.VMEM((SETS, 1, LANES), F32),
            pltpu.VMEM((SETS, NX - 1, HD + 16, RUN), BF),
            pltpu.VMEM((SETS, NX - 1, HD + 16, RUN), BF),
            pltpu.VMEM((SETS, RUN, HD), BF),
            dma((3, SETS)), dma((3, SETS)), dma((3, SETS)), dma,
            dma((2, 2)), dma((2, 2, 2, NY - 1)),
            dma((2,)), dma((2, NY)),
            dma((SETS,)), dma((SETS,)),
            dma((SETS,)), dma((SETS,)),
            dma((SETS,)), dma((SETS,)), dma((SETS,)),
        ],
        compiler_params=pltpu.CompilerParams(
            collective_id=0, has_side_effects=True, vmem_limit_bytes=VMEM_MIB * 1024 * 1024
        ),
    )(queries, keys, values, block_mask)
    whole = pl.BlockSpec(memory_space=pltpu.VMEM)
    return pl.pallas_call(
        arrange,
        out_shape=jax.ShapeDtypeStruct(queries.shape, BF),
        in_specs=[pl.BlockSpec(memory_space=pltpu.SMEM), whole],
        out_specs=whole,
    )(plan, heads)


def solution(mesh):
    placed = (P(("blk", "uly"), None), P(("blk", "uly"), None), P(("blk", "uly"), None), P(), P())
    return jax.shard_map(
        body, mesh=mesh, in_specs=placed, out_specs=P(("blk", "uly"), None), check_vma=False
    )
```

```python
import functools
import math

import jax
import jax.numpy as jnp
from jax import lax
from jax.experimental import pallas as pl
from jax.experimental.pallas import tpu as pltpu
from jax.sharding import PartitionSpec as P

MESH = pl.DeviceIdType.MESH
H, HD, BT, TD = 24, 128, 128, 32
NX, NY, NZ = 4, 4, 8
NB = 64
HL = H // NZ
SETS = 3
RUN = NZ * TD
LANES = NX * RUN
BIG, FLOOR = 1e30, -1e29
VMEM_MIB = 62
NT = (((1,), (1,)), ((), ()))
RATE = math.log2(math.e) / math.sqrt(HD)
BF, F32 = jnp.bfloat16, jnp.float32
K, V, Q = 0, 1, 2


def kernel(
    q_in, k_in, v_in, mask_in, got,
    kb, vb, v_st, q_buf, m_st, shade, acc, top, tot, ob, ob_in, fin,
    us, ur, ul, ml, ys, yr, cs, cr, qs, qr, os_, or_, fs, fr, fl,
):
    u = lax.axis_index("uly")
    b = lax.axis_index("blk")
    core = u % 2
    z = b % NZ
    y = (b // NZ) % NY
    x = (u // 2) * 2 + b // (NZ * NY)

    def at(xx, yy, zz, cc):
        xx, yy, zz = xx % NX, yy % NY, zz % NZ
        return {"uly": (xx // 2) * 2 + cc, "blk": ((xx % 2) * NY + yy) * NZ + zz}

    same = [at(x, y, z + k, core) for k in range(NZ)]
    cross = [at(x, y, z + k, 1 - core) for k in range(NZ)]
    y_side = [at(x, y + d, z, core) for d in range(NY)]
    x_side = [at(x + d, y, z, core) for d in range(NX)]

    barrier = pltpu.get_barrier_semaphore()
    partners = same[1:] + cross + y_side[1:] + x_side[1:]
    for device in partners:
        pl.semaphore_signal(barrier, inc=1, device_id=device, device_id_type=MESH)

    mask_copy = pltpu.make_async_copy(mask_in.at[pl.ds(z * HL, HL)], m_st, ml)
    mask_copy.start()
    here = pl.ds(pl.multiple_of(z * TD, TD), TD)
    sources = (k_in, v_in, q_in)

    def place(a, i):
        if a == V:
            return v_st.at[i, here, :]
        if a == Q:
            return q_buf.at[i, here, :]
        return kb.at[i // 2, 0, i % 2, here, :]

    def columns_of(i, k):
        there = (z + k) % NZ
        lead = (2 * core, 2 - 2 * core, 1)[i]
        return pl.ds(pl.multiple_of((there * HL + lead) * HD, HD), HD)

    def own_in(a, i):
        return pltpu.make_async_copy(sources[a].at[:, columns_of(i, 0)], place(a, i), ul.at[a, i])

    for a in range(3):
        for i in (2, 0):
            own_in(a, i).start()
    pl.semaphore_wait(barrier, len(partners))

    def remote(src, dst, send, recv, device):
        return pltpu.make_async_remote_copy(
            src_ref=src, dst_ref=dst, send_sem=send, recv_sem=recv, device_id=device, device_id_type=MESH
        )

    def sum_of(ref, send, recv):
        return remote(ref, ref, send, recv, same[1])

    far = (4, 3, 5, 2, 6, 1, 7)

    def first_of(i):
        return 0 if i == 1 else 1

    def entry(a, i, k):
        device = cross[k] if i == 1 else same[k]
        return remote(sources[a].at[:, columns_of(i, k)], place(a, i), us.at[a, i], ur.at[a, i], device)

    def entry_all(a, i):
        return sum_of(v_st.at[i, 0:(NZ - first_of(i)) * TD, :], us.at[a, i], ur.at[a, i])

    def send_in(a, i):
        for k in far if i != 1 else far + (0,):
            entry(a, i, k).start()

    def arrive(a, i):
        if i != 1:
            own_in(a, i).wait()
        entry_all(a, i).wait_recv()

    def y_copy(hk, a, half, d):
        buf = vb if a == V else kb
        return remote(
            buf.at[hk, 0, half], buf.at[hk, d, half], ys.at[hk, a], yr.at[hk, a, half, d - 1], y_side[NY - d]
        )

    def y_all(hk, a):
        ref = kb.at[0, 1:NY] if hk == 0 else kb.at[1, 1:NY, 0]
        return sum_of(ref, ys.at[hk, a], yr.at[hk, a, 0, 0])

    def c_copy(a, d):
        buf = vb if a == V else kb
        return remote(buf.at[1, d, 0], buf.at[1, d, 1], cs.at[a], cr.at[a, d], cross[0])

    def c_all(a):
        return sum_of(kb.at[1, 0:NY, 0], cs.at[a], cr.at[a, 0])

    def q_copy(i, d):
        return remote(
            q_buf.at[i, 0:RUN, :], q_buf.at[i, d * RUN:(d + 1) * RUN, :], qs.at[i], qr.at[i], x_side[NX - d]
        )

    def q_all(i):
        return sum_of(q_buf.at[i, RUN:LANES, :], qs.at[i], qr.at[i])

    def o_copy(i, d):
        return remote(ob.at[i, d - 1], ob_in.at[i, d - 1], os_.at[i], or_.at[i], x_side[d])

    def o_all(i):
        return sum_of(ob_in.at[i], os_.at[i], or_.at[i])

    mine = (z * HL + 2 * core, z * HL + 2 * core, z * HL + 1)

    def fin_copy(i, k):
        rows = pl.ds(pl.multiple_of(((z + k) % NZ) * TD, TD), TD)
        device = cross[k] if i == 1 else same[k]
        return remote(fin.at[i, rows, :], got.at[mine[i]], fs.at[i], fr.at[i], device)

    def own_out(i):
        return pltpu.make_async_copy(fin.at[i, here, :], got.at[mine[i]], fl.at[i])

    def fin_all(i):
        return sum_of(got.at[0:NZ - first_of(i)], fs.at[i], fr.at[i])

    def turn(i):
        for n in range(RUN // HD):
            rows = slice(n * HD, (n + 1) * HD)
            vb[i // 2, 0, i % 2, rows, :] = v_st[i, rows, :].T

    def scores(d, half, i, lo):
        return lax.dot_general(kb[i // 2, d, half], q_buf[i, lo:lo + BT, :], NT, preferred_element_type=F32)

    def soften(d, half, i, lo, score, first):
        lanes = slice(lo, lo + BT)
        bias = shade[i // 2, d, :, lanes]
        parts = [score[n * TD:(n + 1) * TD] for n in range(NZ)]
        tops = [jnp.max(p.reshape(TD // 8, 8, BT), axis=0) + bias[n:n + 1] for n, p in enumerate(parts)]
        new_top = jnp.maximum(jnp.max(functools.reduce(jnp.maximum, tops), axis=0, keepdims=True), FLOOR)
        fade = None
        if not first:
            old_top = top[i, :, lanes]
            new_top = jnp.maximum(new_top, old_top)
            fade = jnp.exp2((old_top - new_top) * RATE)
        shift = (bias - new_top) * RATE
        expo = [jnp.exp2(p * RATE + shift[n:n + 1]) for n, p in enumerate(parts)]
        top[i, :, lanes] = new_top
        return jnp.concatenate(expo, axis=0), fade

    def gather(d, half, i, lo, expo, fade):
        lanes = slice(lo, lo + BT)
        vals = jnp.concatenate([vb[i // 2, d, half, n * HD:(n + 1) * HD, :] for n in range(RUN // HD)], axis=1)
        update = jnp.dot(vals, expo.astype(BF), preferred_element_type=F32)
        total = jnp.sum(expo, axis=0, keepdims=True)
        if fade is not None:
            update = update + acc[i, :, lanes] * fade
            total = total + tot[i, :, lanes] * fade
        acc[i, :, lanes] = update
        tot[i, :, lanes] = total

    def unit(parts, first=False):
        todo = [(d, half, i, lo) for d, half, i in parts for lo in range(0, LANES, BT)]
        fresh = len(parts) if first is True else first
        score = scores(*todo[0])
        held = None
        for n, item in enumerate(todo):
            later = scores(*todo[n + 1]) if n + 1 < len(todo) else None
            soft = soften(*item, score, n < fresh * (LANES // BT))
            if held is not None:
                gather(*todo[n - 1], *held)
            held, score = soft, later
        gather(*todo[-1], *held)

    def split3(value):
        terms = []
        for _ in range(3):
            term = value.astype(BF).astype(F32)
            terms.append(term)
            value = value - term
        return terms

    def give_back(i):
        row = lax.broadcasted_iota(jnp.int32, (16, RUN), 0)
        for d in (2, 1, 3):
            lanes = slice(d * RUN, (d + 1) * RUN)
            ob[i, d - 1, 0:HD, :] = acc[i, :, lanes].astype(BF)
            notes = jnp.zeros((16, RUN), F32)
            for n, term in enumerate(split3(top[i, :, lanes]) + split3(tot[i, :, lanes])):
                notes = jnp.where(row == n, term, notes)
            ob[i, d - 1, HD:HD + 16, :] = notes.astype(BF)
            o_copy(i, d).start()

    def combine(i):
        o_all(i).wait_recv()
        own = slice(0, RUN)
        notes = [ob_in[i, d, HD:HD + 16, :].astype(F32) for d in range(NX - 1)]
        tops = [top[i, :, own]] + [n[0:1] + n[1:2] + n[2:3] for n in notes]
        tots = [tot[i, :, own]] + [n[3:4] + n[4:5] + n[5:6] for n in notes]
        best = functools.reduce(jnp.maximum, tops)
        fades = [jnp.exp2((t - best) * RATE) for t in tops]
        share = 1.0 / sum(f * t for f, t in zip(fades, tots))
        mixed = acc[i, :, own] * (fades[0] * share)
        for d in range(NX - 1):
            mixed = mixed + ob_in[i, d, 0:HD, :].astype(F32) * (fades[d + 1] * share)
        fin[i] = mixed.astype(BF).T
        for k in far if i != 1 else far + (0,):
            fin_copy(i, k).start()
        if i != 1:
            own_out(i).start()

    for a in (K, Q, V):
        send_in(a, 0)
        send_in(a, 1)
    for a in (K, V, Q):
        send_in(a, 2)

    for i in (0, 1):
        arrive(K, i)
        for d in (2, 1, 3):
            y_copy(0, K, i, d).start()
    for i in (0, 1):
        arrive(Q, i)
        for d in (2, 1, 3):
            q_copy(i, d).start()
    for i in (0, 1):
        arrive(V, i)
        turn(i)
        for d in (2, 1, 3):
            y_copy(0, V, i, d).start()
    arrive(K, 2)
    for d in (2, 1, 3):
        y_copy(1, K, 0, d).start()
    c_copy(K, 0).start()
    arrive(V, 2)
    turn(2)
    for d in (2, 1, 3):
        y_copy(1, V, 0, d).start()
    c_copy(V, 0).start()
    arrive(Q, 2)
    for d in (2, 1, 3):
        q_copy(2, d).start()

    mask_copy.wait()
    key_row = lax.broadcasted_iota(jnp.int32, (NY * NZ, NB), 0)
    key_col = lax.broadcasted_iota(jnp.int32, (NY * NZ, NB), 1)
    key_block = ((x % 2) * NY + (y + key_row // NZ) % NY) * NZ + key_row % NZ
    pick_key = (key_col == key_block).astype(F32).astype(BF)
    run_row = lax.broadcasted_iota(jnp.int32, (NB, LANES), 0)
    run_col = lax.broadcasted_iota(jnp.int32, (NB, LANES), 1)
    run_block = (((x + run_col // RUN) % 2) * NY + y) * NZ + (run_col // TD) % NZ
    pick_run = (run_row == run_block).astype(F32).astype(BF)
    for hk in range(2):
        allowed = (m_st[2 * core if hk == 0 else 1] > 0).astype(F32).astype(BF)
        rows = lax.dot_general(pick_key, allowed, NT, preferred_element_type=F32).astype(BF)
        rows = jnp.dot(rows, pick_run, preferred_element_type=F32)
        rows = jnp.where(rows > 0.5, 0.0, -BIG)
        for d in range(NY):
            shade[hk, d] = rows[d * NZ:(d + 1) * NZ, :]

    for i in (0, 1):
        q_all(i).wait_recv()
        unit([(0, half, i) for half in (0, 1)], first=1)
    for half, d in ((0, 2), (0, 1), (0, 3), (1, 2)):
        y_copy(0, K, half, d).wait_recv()
        y_copy(0, V, half, d).wait_recv()
        unit([(d, half, i) for i in (0, 1)])
    for d in (1, 3):
        y_copy(0, K, 1, d).wait_recv()
        y_copy(0, V, 1, d).wait_recv()
    for i in (0, 1):
        unit([(d, 1, i) for d in (1, 3)])
        give_back(i)
    for d in (2, 1, 3):
        y_copy(1, K, 0, d).wait_recv()
        c_copy(K, d).start()
    q_all(2).wait_recv()
    for a in (K, V):
        c_copy(a, 0).wait_recv()
    unit([(0, 0, 2), (0, 1, 2)], first=1)
    for d in (2, 1, 3):
        y_copy(1, V, 0, d).wait_recv()
        c_copy(V, d).start()
    unit([(d, 0, 2) for d in (2, 1, 3)])
    for d in (2, 1, 3):
        for a in (K, V):
            c_copy(a, d).wait_recv()
    unit([(d, 1, 2) for d in (2, 1, 3)])
    give_back(2)
    combine(0)
    combine(1)
    for i in range(SETS):
        for a in range(3):
            entry_all(a, i).wait_send()
        q_all(i).wait_send()
    for a in (K, V):
        y_all(0, a).wait_send()
        y_all(1, a).wait_send()
        c_all(a).wait_send()
    combine(2)
    for i in range(SETS):
        o_all(i).wait_send()
    for i in range(SETS):
        fin_all(i).wait_recv()
    for i in range(SETS):
        fin_all(i).wait_send()
        if i != 1:
            own_out(i).wait()


def arrange(plan_s, heads, out):
    for s in range(H):
        out[:, s * HD:(s + 1) * HD] = heads[plan_s[s]]


def body(queries, keys, values, block_mask, plan):
    dma = pltpu.SemaphoreType.DMA
    hbm = pl.BlockSpec(memory_space=pl.ANY)
    heads = pl.pallas_call(
        kernel,
        out_shape=jax.ShapeDtypeStruct((H, TD, HD), BF),
        in_specs=[hbm, hbm, hbm, hbm],
        out_specs=hbm,
        scratch_shapes=[
            pltpu.VMEM((2, NY, 2, RUN, HD), BF),
            pltpu.VMEM((2, NY, 2, RUN, HD), BF),
            pltpu.VMEM((SETS, RUN, HD), BF),
            pltpu.VMEM((SETS, LANES, HD), BF),
            pltpu.VMEM((HL, NB, NB), jnp.int32),
            pltpu.VMEM((2, NY, NZ, LANES), F32),
            pltpu.VMEM((SETS, HD, LANES), F32),
            pltpu.VMEM((SETS, 1, LANES), F32),
            pltpu.VMEM((SETS, 1, LANES), F32),
            pltpu.VMEM((SETS, NX - 1, HD + 16, RUN), BF),
            pltpu.VMEM((SETS, NX - 1, HD + 16, RUN), BF),
            pltpu.VMEM((SETS, RUN, HD), BF),
            dma((3, SETS)), dma((3, SETS)), dma((3, SETS)), dma,
            dma((2, 2)), dma((2, 2, 2, NY - 1)),
            dma((2,)), dma((2, NY)),
            dma((SETS,)), dma((SETS,)),
            dma((SETS,)), dma((SETS,)),
            dma((SETS,)), dma((SETS,)), dma((SETS,)),
        ],
        compiler_params=pltpu.CompilerParams(
            collective_id=0, has_side_effects=True, vmem_limit_bytes=VMEM_MIB * 1024 * 1024
        ),
    )(queries, keys, values, block_mask)
    whole = pl.BlockSpec(memory_space=pltpu.VMEM)
    return pl.pallas_call(
        arrange,
        out_shape=jax.ShapeDtypeStruct(queries.shape, BF),
        in_specs=[pl.BlockSpec(memory_space=pltpu.SMEM), whole],
        out_specs=whole,
    )(plan, heads)


def solution(mesh):
    placed = (P(("blk", "uly"), None), P(("blk", "uly"), None), P(("blk", "uly"), None), P(), P())
    return jax.shard_map(
        body, mesh=mesh, in_specs=placed, out_specs=P(("blk", "uly"), None), check_vma=False
    )
```
